32 devices in a mesh: row: 8 (over z, x), col: 4 (over y, core).
Axes of the slice: x: 2, y: 2, z: 4, core: 2. Of those that a mesh axis runs over, the one named last changes fastest.
Arguments:
- window: float32 [4096, 16384], P('row', 'col'), may hold values from -6 to 6
- leaf_vecs: float32 [2, 4096, 128], P(None, ('row', 'col')), may hold values from -0.25 to 0.25
- leaf_t: float32 [2, 1024, 128], P(None, 'row'), may hold values from -0.25 to 0.25
- node_vecs: float32 [2, 1024, 128], P(None, 'row'), may hold values from -0.5 to 0.5
- node_t: float32 [2, 1024, 128], P(None, 'row'), may hold values from -0.25 to 0.25
Outputs:
- updated: float32 [4096, 16384], P('row', 'col')
The draws below stay inside these ranges and needn't reach their ends.
All inputs are finite; a program needn't handle non-finite values.
Results may differ from the reference program's by a relative error of at most 0.0002.
Values sent between devices are 32-bit elements; how exact they have to be, the bound alone decides.
No kernel may reach another device: no remote copies, remote signals or barrier semaphores. Data moves between devices by JAX's collectives and lax.ppermute only.
A program may use at most 64 MiB of HBM per device.

```python
import jax
import jax.numpy as jnp
from jax import lax

NB = 128
NPAN = 2
NCOLS = 16384
MR_DEV = 512
M = 4096
N_ROW = 8


def block_scale(rng, extent, cuts, least, top_value):
    loudness = 1.0
    for position, parts in cuts:
        heights = jax.random.uniform(jax.random.fold_in(jax.random.fold_in(rng, 6), position), (parts,), jnp.float32, least / len(cuts), top_value / len(cuts))
        loudness = loudness * jnp.repeat(jnp.exp(heights), extent[position] // parts).reshape((-1,) + (1,) * (len(extent) - 1 - position))
    return loudness


def scatter_about(own_key, dims, width, bound, pieces=(), held_as=jnp.bfloat16):
    values = width * jax.random.normal(own_key, dims, jnp.float32)
    if pieces:
        values = values * block_scale(own_key, dims, pieces, -0.22, 0.18)
    return jnp.clip(values, -bound, bound).astype(held_as)


def setup_inputs(seed: int = 0) -> dict:
    arg_keys = jax.random.split(jax.random.key(seed), 6)
    return {
        "window": scatter_about(arg_keys[0], (M, NCOLS), 1.0, 6.0, ((0, 8), (1, 4)), jnp.float32),
        "leaf_vecs": scatter_about(arg_keys[1], (NPAN, M, NB), MR_DEV ** -0.5, 0.25, ((1, 32),), jnp.float32),
        "leaf_t": scatter_about(arg_keys[2], (NPAN, N_ROW * NB, NB), (4 * NB) ** -0.5, 0.25, ((1, 8),), jnp.float32),
        "node_vecs": scatter_about(arg_keys[3], (NPAN, N_ROW * NB, NB), NB ** -0.5, 0.5, ((1, 8),), jnp.float32),
        "node_t": scatter_about(arg_keys[4], (NPAN, N_ROW * NB, NB), (4 * NB) ** -0.5, 0.25, ((1, 8),), jnp.float32),
    }


def matmul(left, right):
    return jnp.dot(left, right, precision=lax.Precision.HIGHEST, preferred_element_type=jnp.float32)


def bmm(form, left, right):
    return jnp.einsum(form, left, right, precision=lax.Precision.HIGHEST)


def reference(window, leaf_vecs, leaf_t, node_vecs, node_t):
    levels = N_ROW.bit_length() - 1
    blocks = window.reshape(N_ROW, MR_DEV, NCOLS)
    for panel in range(NPAN):
        vecs = leaf_vecs[panel].reshape(N_ROW, MR_DEV, NB)
        lfac = leaf_t[panel].reshape(N_ROW, NB, NB)
        nvec = node_vecs[panel].reshape(N_ROW, NB, NB)
        nfac = node_t[panel].reshape(N_ROW, NB, NB)
        inner = bmm("rmk,rmn->rkn", vecs, blocks)
        inner = bmm("rjk,rjn->rkn", lfac, inner)
        blocks = blocks - bmm("rmk,rkn->rmn", vecs, inner)
        tops = blocks[:, :NB, :]
        for level in range(levels):
            stride = 1 << level
            lower_list = [index for index in range(N_ROW) if (index >> level) % 2 == 0]
            lower_ids = jnp.array(lower_list, dtype=jnp.int32)
            upper_ids = lower_ids + stride
            top_a = tops[lower_ids]
            top_b = tops[upper_ids]
            vb = nvec[upper_ids]
            sb = nfac[upper_ids]
            weight = top_a + bmm("rjk,rjn->rkn", vb, top_b)
            weight = bmm("rjk,rjn->rkn", sb, weight)
            tops = tops.at[lower_ids].set(top_a - weight)
            tops = tops.at[upper_ids].set(top_b - bmm("rkj,rjn->rkn", vb, weight))
        root = tops[0]
        inner = matmul(nvec[0].T, root)
        inner = matmul(nfac[0].T, inner)
        tops = tops.at[0].set(root - matmul(nvec[0], inner))
        blocks = jnp.concatenate([tops, blocks[:, NB:, :]], axis=1)
    return blocks.reshape(M, NCOLS)
```

```python
import functools

import jax
import jax.numpy as jnp
from jax import lax
from jax.experimental import pallas as pl
from jax.experimental.pallas import tpu as pltpu
from jax.sharding import PartitionSpec as P

VMEM_LIMIT = 24 * 1024 * 1024
F32 = jnp.float32
BF16 = jnp.bfloat16


def mm(left, right):
    return jnp.dot(left, right, precision=lax.Precision.HIGHEST, preferred_element_type=F32)


def halves(value):
    high = value.astype(BF16)
    return high, (value - high.astype(F32)).astype(BF16)


def mm3(left, right):
    high, low = halves(right)

    def dot(a, b):
        return jnp.dot(a, b, preferred_element_type=F32)

    return dot(left[0], high) + (dot(left[0], low) + dot(left[1], high))


def params():
    return pltpu.CompilerParams(vmem_limit_bytes=VMEM_LIMIT)


def cost(flops, nbytes):
    return pl.CostEstimate(flops=int(flops), bytes_accessed=int(nbytes), transcendentals=0)


def prep_kernel(vecs_ref, leaf_ref, rows_ref, send_ref, rest_ref, dmat_ref):
    width = leaf_ref.shape[-1]

    def put(ref, place, value):
        high, low = halves(value)
        ref[(0, *place)] = high
        ref[(1, *place)] = low

    one, two = vecs_ref[0], vecs_ref[1]
    one_top, one_rest = one[:width], one[width:]
    two_top, two_rest = two[:width], two[width:]
    first, second = leaf_ref[0].T, leaf_ref[1].T
    two_rest_t, two_top_t = two_rest.T, two_top.T
    zero = jnp.zeros((width, width), F32)
    left, right, both = slice(0, width), slice(width, 2 * width), slice(None)
    cross = mm(two_rest_t, one_rest)
    lower = -mm(second, mm(cross, first))
    top_l, rest_l = mm(two_top, second), mm(two_rest, second)
    put(rows_ref, (left, both), one.T)
    put(rows_ref, (right, left), zero)
    put(rows_ref, (right, slice(width, None)), two_rest_t)
    put(send_ref, (left, left), -mm(one_top, first))
    put(send_ref, (left, right), zero)
    put(send_ref, (right, left), mm(two_top, lower))
    put(send_ref, (right, right), top_l)
    put(rest_ref, (both, left), mm(one_rest, first) + mm(two_rest, lower))
    put(rest_ref, (both, right), rest_l)
    put(rest_ref, (both, slice(2 * width, None)), mm(rest_l, two_top_t))
    shape = (width, width)
    eye = lax.broadcasted_iota(jnp.int32, shape, 0) == lax.broadcasted_iota(jnp.int32, shape, 1)
    dmat_ref[...] = eye.astype(F32) - mm(top_l, two_top_t)


def pack_kernel(place_ref, vecs_ref, t_ref, dmat_ref, after_ref, out_ref):
    share = out_ref.shape[1]
    part = pl.ds(pl.multiple_of(place_ref[1] * share, share), share)
    for panel in range(vecs_ref.shape[0]):
        out_ref[2 * panel] = vecs_ref[panel, part, :]
        out_ref[2 * panel + 1] = t_ref[panel, part, :]
    out_ref[2 * vecs_ref.shape[0]] = dmat_ref[part, :]


def leaf_kernel(place_ref, window_ref, rows_ref, send_ref, after_ref, inner_ref, *pieces):
    width = send_ref.shape[1] // 2
    inner = mm3((rows_ref[0], rows_ref[1]), window_ref[...])
    inner_ref[0] = inner
    message = mm3((send_ref[0], send_ref[1]), inner)
    top = message[:width] + window_ref[:width, :]
    for i, piece in enumerate(pieces):

        @pl.when(pl.program_id(0) == i)
        def _(piece=piece):
            piece[:width, :] = top
            piece[width:, :] = message[width:]


def nodes_kernel(place_ref, pack_ref, pair_ref, dmat_ref):
    width, cols = pack_ref.shape[-1], pack_ref.shape[1]
    col = place_ref[1]

    def whole(i):
        return jnp.concatenate([pack_ref[0, c ^ col, i] for c in range(cols)], axis=0)

    def put(panel, rows, columns, value):
        high, low = halves(value)
        pair_ref[0, panel, 0, rows, columns] = high
        pair_ref[1, panel, 0, rows, columns] = low

    top, low = slice(0, width), slice(width, 2 * width)
    panels = pair_ref.shape[1]
    for panel in range(panels):
        vfac = whole(2 * panel)
        sfac_t = whole(2 * panel + 1).T
        right = mm(sfac_t, vfac.T)
        put(panel, top, top, sfac_t)
        put(panel, top, low, right)
        put(panel, low, top, mm(vfac, sfac_t))
        put(panel, low, low, mm(vfac, right))
    dmat_ref[0, 0], dmat_ref[1, 0] = halves(whole(2 * panels))


def tree_kernel(rows, order, place_ref, pair_ref, dmat_ref, *refs):
    pieces, outs = [None] * rows, [None] * rows
    for i, k in enumerate(order):
        pieces[k] = refs[i]
        outs[k] = refs[rows + i]
    first, second = refs[2 * rows :]
    width = first.shape[1]
    me = place_ref[0]
    levels = rows.bit_length() - 1
    for k in range(rows):
        first[me ^ k] = pieces[k][:width, :]
        second[me ^ k] = pieces[k][width:, :]

    def each(count, body):
        if rows <= 8:
            for j in range(count):
                body(j, 0)
        else:
            lax.fori_loop(0, count, body, 0)

    def sweep(panel, tops):
        for level in range(levels):
            stride = 1 << level

            def pair(j, carry, level=level, stride=stride):
                a = (j >> level << (level + 1)) + (j & (stride - 1))
                b = a + stride
                top_a, top_b = tops[a], tops[b]
                both = jnp.concatenate([top_a, top_b], axis=0)
                change = mm3((pair_ref[0, panel, b], pair_ref[1, panel, b]), both)
                tops[a] = top_a - change[:width]
                tops[b] = top_b - change[width:]
                return carry

            each(rows // 2, pair)
        root = tops[0]
        low = slice(width, 2 * width)
        tops[0] = root - mm3((pair_ref[0, panel, 0, low, low], pair_ref[1, panel, 0, low, low]), root)

    def leaf(r, carry):
        second[r] = mm3((dmat_ref[0, r], dmat_ref[1, r]), first[r]) - second[r]
        return carry

    sweep(0, first)
    each(rows, leaf)
    sweep(1, second)
    for k in range(rows):
        outs[k][:width, :] = first[me ^ k]
        outs[k][width:, :] = second[me ^ k]


def last_kernel(count, place_ref, window_ref, inner_ref, rest_ref, *refs):
    pieces = refs[:count]
    out_ref, both = refs[-2], refs[-1]
    width = inner_ref.shape[1] // 2
    both[: 2 * width, :] = inner_ref[0]
    for i, piece in enumerate(pieces):

        @pl.when(pl.program_id(0) == i)
        def _(piece=piece):
            both[2 * width :, :] = piece[:width, :]
            out_ref[:width, :] = piece[width:, :]

    out_ref[width:, :] = window_ref[width:, :] - mm3((rest_ref[0], rest_ref[1]), both[...])


def vmem():
    return pl.BlockSpec(memory_space=pltpu.VMEM)


def anywhere():
    return pl.BlockSpec(memory_space=pl.ANY)


def smem():
    return pl.BlockSpec(memory_space=pltpu.SMEM)


def held(shape):
    return pl.BlockSpec(shape, lambda i, place: (0,) * len(shape))


def swap(value, axis, k):
    return lax.ppermute(value, axis, [(i, i ^ k) for i in range(lax.axis_size(axis))])


def local(window, leaf_vecs, leaf_t, node_vecs, node_t):
    rows, cols = lax.axis_size("row"), lax.axis_size("col")
    width = leaf_t.shape[-1]
    panels = leaf_t.shape[0]
    height, ncols = window.shape
    chunks = 2 if ncols % (2 * rows * 128) == 0 else 1
    span = ncols // chunks
    n = span // rows
    aligned = n % 128 == 0
    me = lax.axis_index("row").astype(jnp.int32)
    col = lax.axis_index("col").astype(jnp.int32)
    place = jnp.stack([me, col])

    vecs = lax.all_gather(leaf_vecs, "col", axis=1, tiled=True)
    rows_m, send_m, rest_m, dmat = pl.pallas_call(
        prep_kernel,
        out_shape=(
            jax.ShapeDtypeStruct((2, 2 * width, height), BF16),
            jax.ShapeDtypeStruct((2, 2 * width, 2 * width), BF16),
            jax.ShapeDtypeStruct((2, height - width, 3 * width), BF16),
            jax.ShapeDtypeStruct((width, width), F32),
        ),
        in_specs=[vmem(), vmem()],
        out_specs=(vmem(),) * 4,
        compiler_params=params(),
        cost_estimate=cost(40 * width**3 * 6, 2**21),
        name="prep",
    )(vecs, leaf_t)

    if aligned:
        source = window

        def columns(chunk, k0):
            return pl.BlockSpec((height, n), lambda i, place: (0, chunk * rows + (place[0] ^ (k0 + i))))

        out_shape = jax.ShapeDtypeStruct(window.shape, F32)
    else:
        source = jnp.stack([lax.dynamic_slice_in_dim(window, (me ^ k) * n, n, axis=1) for k in range(rows)])

        def columns(chunk, k0):
            return pl.BlockSpec((None, height, n), lambda i, place: (k0 + i, 0, 0))

        out_shape = jax.ShapeDtypeStruct(source.shape, F32)

    def leaf(chunk, k0, count, after):
        out = pl.pallas_call(
            leaf_kernel,
            grid_spec=pltpu.PrefetchScalarGridSpec(
                num_scalar_prefetch=1,
                grid=(count,),
                in_specs=[columns(chunk, k0), held(rows_m.shape), held(send_m.shape), anywhere()],
                out_specs=(pl.BlockSpec((1, 2 * width, n), lambda i, place: (i, 0, 0)),)
                + (held((2 * width, n)),) * count,
            ),
            out_shape=(jax.ShapeDtypeStruct((count, 2 * width, n), F32),)
            + (jax.ShapeDtypeStruct((2 * width, n), F32),) * count,
            compiler_params=params(),
            cost_estimate=cost(
                2 * 2 * width * (height + 2 * width) * n * count * 3, 4 * n * count * (height + 4 * width)
            ),
            name="leaf",
        )(place, source, rows_m, send_m, after)
        return out[0], list(out[1:])

    def tree(pieces):
        out = pl.pallas_call(
            functools.partial(tree_kernel, rows, order),
            out_shape=(jax.ShapeDtypeStruct((2 * width, n), F32),) * rows,
            in_specs=[smem()] + [vmem()] * (2 + rows),
            out_specs=(vmem(),) * rows,
            scratch_shapes=[pltpu.VMEM((rows, width, n), F32)] * 2,
            compiler_params=params(),
            cost_estimate=cost(rows * 8 * 4 * width * width * n * 3, 2**23),
            name="tree",
        )(place, pairs, dmats, *[pieces[k] for k in order])
        return [out[order.index(k)] for k in range(rows)]

    def last(chunk, k0, inner, pieces, out):
        count = len(pieces)
        in_specs = [
            columns(chunk, k0),
            pl.BlockSpec((1, 2 * width, n), lambda i, place: (i, 0, 0)),
            held(rest_m.shape),
        ] + [held((2 * width, n))] * count
        operands = [place, source, inner, rest_m, *pieces]
        aliases = {}
        if out is not None:
            in_specs.append(pl.BlockSpec(memory_space=pl.ANY))
            aliases = {len(operands): 0}
            operands.append(out)
        return pl.pallas_call(
            functools.partial(last_kernel, count),
            grid_spec=pltpu.PrefetchScalarGridSpec(
                num_scalar_prefetch=1,
                grid=(count,),
                in_specs=in_specs,
                out_specs=columns(chunk, k0),
                scratch_shapes=[pltpu.VMEM((3 * width, n), F32)],
            ),
            out_shape=out_shape,
            input_output_aliases=aliases,
            compiler_params=params(),
            cost_estimate=cost(
                2 * 3 * width * (height - width) * n * count * 3, 4 * n * count * (2 * height + 4 * width)
            ),
            name="last",
        )(*operands)

    half = rows // 2
    groups = [(half, rows - half), (0, half)]
    inners, sent, after = {}, [], send_m
    for chunk in range(chunks):
        made = [None] * rows
        for k0, count in groups:
            after, made[k0 : k0 + count] = leaf(chunk, k0, count, after)
            inners[chunk, k0] = after
        sent.append(made)
    order = [half + 0, half + 1]
    for k in range(1, half):
        order += [k] + ([half + 1 + k] if half + 1 + k < rows else [])
    order = order[:] + [0]

    def trade(pieces):
        got = list(pieces)
        for k in order[:-1]:
            got[k] = swap(pieces[k], "row", k)
        return got

    arrived = [trade(pieces) for pieces in sent]
    share = width // cols
    pack = pl.pallas_call(
        pack_kernel,
        out_shape=jax.ShapeDtypeStruct((2 * panels + 1, share, width), F32),
        in_specs=[smem(), vmem(), vmem(), vmem(), anywhere()],
        out_specs=vmem(),
        compiler_params=params(),
        cost_estimate=cost(0, 2**20),
        name="pack",
    )(place, node_vecs, node_t, dmat, arrived[0][order[0]])
    pack = pack[None]
    for k in [1 << bit for bit in reversed(range(rows.bit_length() - 1))]:
        pack = jnp.stack([pack, swap(pack, "row", k)], axis=1)
        pack = pack.reshape(-1, *pack.shape[2:])
    pack = pack[:, None]
    for k in [1 << bit for bit in reversed(range(cols.bit_length() - 1))]:
        pack = jnp.stack([pack, swap(pack, "col", k)], axis=2)
        pack = pack.reshape(rows, -1, *pack.shape[3:])
    pairs, dmats = pl.pallas_call(
        nodes_kernel,
        grid_spec=pltpu.PrefetchScalarGridSpec(
            num_scalar_prefetch=1,
            grid=(rows,),
            in_specs=[
                pl.BlockSpec((1, *pack.shape[1:]), lambda r, place: (r ^ place[0], 0, 0, 0, 0)),
            ],
            out_specs=(
                pl.BlockSpec((2, panels, 1, 2 * width, 2 * width), lambda r, place: (0, 0, r, 0, 0)),
                pl.BlockSpec((2, 1, width, width), lambda r, place: (0, r, 0, 0)),
            ),
        ),
        out_shape=(
            jax.ShapeDtypeStruct((2, panels, rows, 2 * width, 2 * width), BF16),
            jax.ShapeDtypeStruct((2, rows, width, width), BF16),
        ),
        compiler_params=params(),
        cost_estimate=cost(rows * 12 * width**3 * 6, 2**23),
        name="nodes",
    )(place, pack)

    returned = [trade(tree(pieces)) for pieces in arrived]
    out = None
    for chunk in range(chunks):
        for k0, count in reversed(groups):
            out = last(chunk, k0, inners[chunk, k0], returned[chunk][k0 : k0 + count], out)
    if aligned:
        return out
    result = jnp.zeros(window.shape, F32)
    for k in range(rows):
        result = lax.dynamic_update_slice_in_dim(result, out[k], (me ^ k) * n, axis=1)
    return result


def solution(mesh):
    placed = (
        P("row", "col"),
        P(None, ("row", "col"), None),
        P(None, "row", None),
        P(None, "row", None),
        P(None, "row", None),
    )
    return jax.shard_map(
        local, mesh=mesh, in_specs=placed, out_specs=P("row", "col"), check_vma=False
    )
```

```python
import functools

import jax
import jax.numpy as jnp
from jax import lax
from jax.experimental import pallas as pl
from jax.experimental.pallas import tpu as pltpu
from jax.sharding import PartitionSpec as P

VMEM_LIMIT = 16 * 1024 * 1024
LARGE_LIMIT = 56 * 1024 * 1024
F32 = jnp.float32
BF16 = jnp.bfloat16
FLIGHT = 3
STRICT = False
RIDE = 0
PACE = (0, 2, 4)
CHUNKS = 2


def mm(left, right):
    return jnp.dot(left, right, precision=lax.Precision.HIGHEST, preferred_element_type=F32)


def halves(value):
    high = value.astype(BF16)
    return high, (value - high.astype(F32)).astype(BF16)


def mm3(left, right):
    high, low = halves(right)

    def dot(a, b):
        return jnp.dot(a, b, preferred_element_type=F32)

    return dot(left[0], high) + (dot(left[0], low) + dot(left[1], high))


def params(limit=VMEM_LIMIT):
    return pltpu.CompilerParams(vmem_limit_bytes=limit)


def cost(flops, nbytes):
    return pl.CostEstimate(flops=int(flops), bytes_accessed=int(nbytes), transcendentals=0)


def prep_kernel(vecs_ref, leaf_ref, after_ref, rows_ref, send_ref, rest_ref, dmat_ref):
    width = leaf_ref.shape[-1]

    def put(ref, place, value):
        high, low = halves(value)
        ref[(0, *place)] = high
        ref[(1, *place)] = low

    one, two = vecs_ref[0], vecs_ref[1]
    one_top, one_rest = one[:width], one[width:]
    two_top, two_rest = two[:width], two[width:]
    first, second = leaf_ref[0].T, leaf_ref[1].T
    two_rest_t, two_top_t = two_rest.T, two_top.T
    zero = jnp.zeros((width, width), F32)
    left, right, both = slice(0, width), slice(width, 2 * width), slice(None)
    cross = mm(two_rest_t, one_rest)
    lower = -mm(second, mm(cross, first))
    top_l, rest_l = mm(two_top, second), mm(two_rest, second)
    put(rows_ref, (left, both), one.T)
    put(rows_ref, (right, left), zero)
    put(rows_ref, (right, slice(width, None)), two_rest_t)
    put(send_ref, (left, left), -mm(one_top, first))
    put(send_ref, (left, right), zero)
    put(send_ref, (right, left), mm(two_top, lower))
    put(send_ref, (right, right), top_l)
    put(rest_ref, (both, left), mm(one_rest, first) + mm(two_rest, lower))
    put(rest_ref, (both, right), rest_l)
    put(rest_ref, (both, slice(2 * width, None)), mm(rest_l, two_top_t))
    shape = (width, width)
    eye = lax.broadcasted_iota(jnp.int32, shape, 0) == lax.broadcasted_iota(jnp.int32, shape, 1)
    dmat_ref[...] = eye.astype(F32) - mm(top_l, two_top_t)


def pack_kernel(place_ref, vecs_ref, t_ref, out_ref):
    panels = vecs_ref.shape[0]
    share = out_ref.shape[1] // (2 * panels)
    part = pl.ds(pl.multiple_of(place_ref[1] * share, share), share)
    for panel in range(panels):
        out_ref[0, pl.ds(2 * panel * share, share), :] = vecs_ref[panel, part, :]
        out_ref[0, pl.ds((2 * panel + 1) * share, share), :] = t_ref[panel, part, :]


def touch_kernel(*refs):
    refs[-1][...] = refs[0][...]


def leaf_kernel(parts, place_ref, window_ref, rows_ref, send_ref, after_ref, inner_ref, *refs):
    pieces, (buffer, sems) = refs[: len(parts)], refs[len(parts) :]
    width = send_ref.shape[1] // 2
    copies = []
    for i, part in enumerate(parts):
        copy = pltpu.make_async_copy(part(place_ref, window_ref), buffer.at[i], sems.at[i])
        copy.start()
        copies.append(copy)
    for i, piece in enumerate(pieces):
        copies[i].wait()
        inner = mm3((rows_ref[0], rows_ref[1]), buffer[i])
        inner_ref[i] = inner
        message = mm3((send_ref[0], send_ref[1]), inner)
        piece[:width, :] = message[:width] + buffer[i, :width, :]
        piece[width:, :] = message[width:]


def nodes_kernel(place_ref, after_ref, pack_ref, pair_ref):
    width = pair_ref.shape[-1] // 2

    def whole(i):
        parts = pack_ref.shape[0]
        share = width // parts
        return jnp.concatenate(
            [pack_ref[c ^ place_ref[1], 0, i * share : (i + 1) * share] for c in range(parts)], axis=0
        )

    def put(panel, rows, columns, value):
        high, low = halves(value)
        pair_ref[0, panel, 0, rows, columns] = high
        pair_ref[1, panel, 0, rows, columns] = low

    top, low = slice(0, width), slice(width, 2 * width)
    panels = pair_ref.shape[1]
    for panel in range(panels):
        vfac = whole(2 * panel)
        sfac_t = whole(2 * panel + 1).T
        right = mm(sfac_t, vfac.T)
        put(panel, top, top, sfac_t)
        put(panel, top, low, right)
        put(panel, low, top, mm(vfac, sfac_t))
        put(panel, low, low, mm(vfac, right))


def tree_kernel(rows, order, place_ref, pair_ref, dmat_ref, *refs):
    pieces, outs = [None] * rows, [None] * rows
    for i, k in enumerate(order):
        pieces[k] = refs[i]
        outs[k] = refs[rows + i]
    first, second = refs[2 * rows :]
    width = first.shape[1]
    me = place_ref[0]
    levels = rows.bit_length() - 1
    for k in range(rows):
        first[me ^ k] = pieces[k][:width, :]
        second[me ^ k] = pieces[k][width:, :]

    def each(count, body):
        if rows <= 8:
            for j in range(count):
                body(j, 0)
        else:
            lax.fori_loop(0, count, body, 0)

    def sweep(panel, tops):
        for level in range(levels):
            stride = 1 << level

            def pair(j, carry, level=level, stride=stride):
                a = (j >> level << (level + 1)) + (j & (stride - 1))
                b = a + stride
                top_a, top_b = tops[a], tops[b]
                both = jnp.concatenate([top_a, top_b], axis=0)
                change = mm3((pair_ref[0, panel, b], pair_ref[1, panel, b]), both)
                tops[a] = top_a - change[:width]
                tops[b] = top_b - change[width:]
                return carry

            each(rows // 2, pair)
        root = tops[0]
        low = slice(width, 2 * width)
        tops[0] = root - mm3((pair_ref[0, panel, 0, low, low], pair_ref[1, panel, 0, low, low]), root)

    def leaf(r, carry):
        dmat = jnp.concatenate([dmat_ref[c ^ place_ref[1], me ^ r] for c in range(dmat_ref.shape[0])], axis=0)
        second[r] = mm3(halves(dmat), first[r]) - second[r]
        return carry

    sweep(0, first)
    each(rows, leaf)
    sweep(1, second)
    for k in range(rows):
        outs[k][:width, :] = first[me ^ k]
        outs[k][width:, :] = second[me ^ k]


def last_kernel(parts, begin, place_ref, window_ref, inner_ref, rest_ref, *refs):
    count = len(parts)
    pieces, (out_ref, buffer, both, sems) = refs[:count], refs[-4:]
    width = inner_ref.shape[1] // 2
    loads, stores = [], []
    for i, part in enumerate(parts):
        source = part(place_ref, window_ref).at[pl.ds(width, window_ref.shape[-2] - width)]
        loads.append(pltpu.make_async_copy(source, buffer.at[i, pl.ds(width, source.shape[0])], sems.at[0, i]))
        stores.append(pltpu.make_async_copy(buffer.at[i], part(place_ref, out_ref), sems.at[1, i]))
    for load in loads:
        load.start()
    for i, piece in enumerate(pieces):
        both[: 2 * width, :] = inner_ref[begin + i]
        both[2 * width :, :] = piece[:width, :]
        change = mm3((rest_ref[0], rest_ref[1]), both[...])
        buffer[i, :width, :] = piece[width:, :]
        loads[i].wait()
        buffer[i, width:, :] = buffer[i, width:, :] - change
        stores[i].start()
    for store in stores:
        store.wait()


def vmem():
    return pl.BlockSpec(memory_space=pltpu.VMEM)


def anywhere():
    return pl.BlockSpec(memory_space=pl.ANY)


def smem():
    return pl.BlockSpec(memory_space=pltpu.SMEM)


def hbm():
    return pl.BlockSpec(memory_space=pltpu.HBM)


def swap(value, axis, k):
    return lax.ppermute(value, axis, [(i, i ^ k) for i in range(lax.axis_size(axis))])


def butterfly(window, leaf_vecs, leaf_t, node_vecs, node_t):
    width, panels = leaf_t.shape[-1], leaf_t.shape[0]
    rows = lax.axis_size("row")
    me = lax.axis_index("row")
    work = window
    all_rows = lax.all_gather(leaf_vecs, "col", axis=1, tiled=True)
    for panel in range(panels):
        vecs = all_rows[panel]
        work = work - mm(vecs, mm(leaf_t[panel].T, mm(vecs.T, work)))
        top, vfac, sfac = work[:width], node_vecs[panel], node_t[panel]
        for level in range(rows.bit_length() - 1):
            lower = me // (1 << level) % 2 == 0
            got, got_v, got_s = (swap(value, "row", 1 << level) for value in (top, vfac, sfac))
            top_a, top_b = jnp.where(lower, top, got), jnp.where(lower, got, top)
            use_v, use_s = jnp.where(lower, got_v, vfac), jnp.where(lower, got_s, sfac)
            weight = mm(use_s.T, top_a + mm(use_v.T, top_b))
            top = jnp.where(lower, top_a - weight, top_b - mm(use_v, weight))
        root = top - mm(vfac, mm(sfac.T, mm(vfac.T, top)))
        work = jnp.concatenate([jnp.where(me == 0, root, top), work[width:]], axis=0)
    return work


def local(window, leaf_vecs, leaf_t, node_vecs, node_t):
    rows, cols = lax.axis_size("row"), lax.axis_size("col")
    width = leaf_t.shape[-1]
    panels = leaf_t.shape[0]
    height, ncols = window.shape
    chunks = CHUNKS if ncols % (CHUNKS * rows * 128) == 0 else 1
    span = ncols // chunks
    n = span // rows
    if n % 128 or panels != 2 or rows < 4:
        return butterfly(window, leaf_vecs, leaf_t, node_vecs, node_t)
    me = lax.axis_index("row").astype(jnp.int32)
    col = lax.axis_index("col").astype(jnp.int32)
    parts = 2 if cols % 2 == 0 else 1
    core = col % parts
    place = jnp.stack([me, core])

    vecs = lax.all_gather(leaf_vecs, "col", axis=1, tiled=True)
    share = width // parts
    pack = pl.pallas_call(
        pack_kernel,
        out_shape=jax.ShapeDtypeStruct((1, 2 * panels * share, width), F32),
        in_specs=[smem(), vmem(), vmem()],
        out_specs=vmem(),
        compiler_params=params(),
        cost_estimate=cost(0, 2**20),
        name="pack",
    )(place, node_vecs, node_t)
    steps = []
    for k in [1 << bit for bit in reversed(range(rows.bit_length() - 1))]:
        steps.append(swap(pack, "row", k))
        pack = jnp.stack([pack, steps[-1]], axis=1).reshape(-1, *pack.shape[1:])

    rows_m, send_m, rest_m, dmat = pl.pallas_call(
        prep_kernel,
        out_shape=(
            jax.ShapeDtypeStruct((2, 2 * width, height), BF16),
            jax.ShapeDtypeStruct((2, 2 * width, 2 * width), BF16),
            jax.ShapeDtypeStruct((2, height - width, 3 * width), BF16),
            jax.ShapeDtypeStruct((width, width), F32),
        ),
        in_specs=[vmem(), vmem(), vmem()],
        out_specs=(vmem(),) * 4,
        compiler_params=params(),
        cost_estimate=cost(40 * width**3 * 6, 2**21),
        name="prep",
    )(vecs, leaf_t, steps[0])

    def part(chunk, k):
        return lambda place, ref: ref.at[:, pl.ds(pl.multiple_of((chunk * rows + (place[0] ^ k)) * n, n), n)]

    def touch(value, after):
        if not after:
            return value
        return pl.pallas_call(
            touch_kernel,
            out_shape=jax.ShapeDtypeStruct(value.shape, value.dtype),
            in_specs=[vmem()] * (1 + len(after)),
            out_specs=vmem(),
            input_output_aliases={0: 0},
            compiler_params=params(),
            cost_estimate=cost(0, 0),
            name="touch",
        )(value, *after)

    def leaf(chunk, ks, after):
        count = len(ks)
        out = pl.pallas_call(
            functools.partial(leaf_kernel, [part(chunk, k) for k in ks]),
            in_specs=[smem(), hbm(), vmem(), vmem(), vmem()],
            out_specs=(vmem(),) * (1 + count),
            scratch_shapes=[pltpu.VMEM((count, height, n), F32), pltpu.SemaphoreType.DMA((count,))],
            out_shape=(jax.ShapeDtypeStruct((count, 2 * width, n), F32),)
            + (jax.ShapeDtypeStruct((2 * width, n), F32),) * count,
            compiler_params=params(LARGE_LIMIT if chunk == 0 and ks[0] == far[0] else VMEM_LIMIT),
            cost_estimate=cost(
                2 * 2 * width * (height + 2 * width) * n * count * 3, 4 * n * count * (height + 4 * width)
            ),
            name="leaf",
        )(place, window, rows_m, send_m, after)
        return out[0], list(out[1:])

    def nodes(pack, after):
        return pl.pallas_call(
            nodes_kernel,
            grid_spec=pltpu.PrefetchScalarGridSpec(
                num_scalar_prefetch=1,
                grid=(rows,),
                in_specs=[
                    pl.BlockSpec(after.shape, lambda r, place: (0, 0)),
                    pl.BlockSpec((parts, 1, *pack.shape[2:]), lambda r, place: (0, r ^ place[0], 0, 0)),
                ],
                out_specs=pl.BlockSpec((2, panels, 1, 2 * width, 2 * width), lambda r, place: (0, 0, r, 0, 0)),
            ),
            out_shape=jax.ShapeDtypeStruct((2, panels, rows, 2 * width, 2 * width), BF16),
            compiler_params=params(),
            cost_estimate=cost(rows * 12 * width**3 * 6, 2**23),
            name="nodes",
        )(place, after, pack)

    def tree(pairs, dmats, pieces):
        out = pl.pallas_call(
            functools.partial(tree_kernel, rows, order),
            out_shape=(jax.ShapeDtypeStruct((2 * width, n), F32),) * rows,
            in_specs=[smem()] + [vmem()] * (2 + rows),
            out_specs=(vmem(),) * rows,
            scratch_shapes=[pltpu.VMEM((rows, width, n), F32)] * 2,
            compiler_params=params(),
            cost_estimate=cost(rows * 8 * 4 * width * width * n * 3, 2**23),
            name="tree",
        )(place, pairs, dmats, *[pieces[k] for k in order])
        return [out[order.index(k)] for k in range(rows)]

    def last(chunk, ks, inner, begin, pieces, out):
        count = len(ks)
        operands = [place, window, inner, rest_m, *pieces]
        in_specs = [smem(), hbm()] + [vmem()] * (2 + count)
        aliases = {}
        if out is not None:
            in_specs.append(hbm())
            aliases = {len(operands): 0}
            operands.append(out)
        return pl.pallas_call(
            functools.partial(last_kernel, [part(chunk, k) for k in ks], begin),
            in_specs=in_specs,
            out_specs=hbm(),
            scratch_shapes=[
                pltpu.VMEM((count, height, n), F32),
                pltpu.VMEM((3 * width, n), F32),
                pltpu.SemaphoreType.DMA((2, count)),
            ],
            out_shape=jax.ShapeDtypeStruct(window.shape, F32),
            input_output_aliases=aliases,
            compiler_params=params(),
            cost_estimate=cost(
                2 * 3 * width * (height - width) * n * count * 3, 4 * n * count * (2 * height + 4 * width)
            ),
            name="last",
        )(*operands)

    half = rows // 2
    far, near = list(range(half, rows)), list(range(1, half))
    order = far + near + [0]
    cut = max(1, half // 2)

    inners, sent = {}, [[None] * rows for _ in range(chunks)]

    def leaves(chunk, ks, after):
        inner, made = leaf(chunk, ks, after)
        for i, k in enumerate(ks):
            inners[chunk, k] = inner, i
            sent[chunk][k] = made[i]
        return inner

    ride = far[RIDE]
    flat = share
    groups = max(1, n // width)
    extra = flat * width // n

    def fold(pack):
        return jnp.concatenate([pack[g * extra : (g + 1) * extra] for g in range(groups)], axis=1)

    def unfold(rider):
        return jnp.concatenate([rider[:, g * width : (g + 1) * width] for g in range(groups)], axis=0)

    fars, nears, queue = [], [], []

    def far_swap(value, k):
        needs = fars[len(fars) - FLIGHT :][:1] if len(fars) >= FLIGHT else []
        if STRICT:
            needs += nears[:-1]
            del nears[:-1]
        fars.append(swap(touch(value, needs), "row", k))
        return fars[-1]

    def near_trades(got, pieces):
        def run(k):
            got[k] = swap(pieces[k], "row", k)
            nears.append(got[k])

        return [functools.partial(run, k) for k in near]

    arrived = [[None] * rows for _ in range(chunks)]
    own = other = None
    for chunk in range(chunks):
        if chunk == 0:
            after = leaves(0, far[:cut], send_m)
            leaves(0, far[cut:], steps[min(1, len(steps) - 1)])
        else:
            leaves(chunk, far, fars[0])
            leaves(chunk, [0] + near, fars[0])
            arrived[chunk][0] = sent[chunk][0]
            for k in near:
                arrived[chunk][k] = swap(sent[chunk][k], "row", k)
        for k in far:
            if (chunk, k) == (0, ride):
                own = fold(lax.dynamic_slice_in_dim(dmat, core * share, share, axis=0))
                got = far_swap(jnp.concatenate([sent[0][k], own]), k)
                arrived[0][k], other = got[: 2 * width], got[2 * width :]
                leaves(0, [0] + near, fars[0])
                arrived[0][0] = sent[0][0]
                for j in near:
                    sent[0][j] = jnp.concatenate([sent[0][j], own, other])
                queue += near_trades(arrived[0], sent[0])
            else:
                arrived[chunk][k] = far_swap(sent[chunk][k], k)
            if queue:
                queue.pop(0)()

    while any(got is None for got in arrived[0]):
        queue.pop(0)()
    shares = {0: own, ride: other}
    for k in near:
        got = arrived[0][k]
        arrived[0][k] = got[: 2 * width]
        shares[k], shares[k ^ ride] = got[2 * width : 2 * width + extra], got[2 * width + extra :]
    shares = jnp.stack([unfold(shares[k]) for k in range(rows)])
    def join(value, after):
        if parts == 1:
            return value[None]
        return jnp.stack([value, swap(touch(value, after), "col", 1)])

    pace = [fars[min(i, len(fars) - 1)] for i in PACE]
    dmats = join(shares, [pace[2]])
    pack = join(pack, [pace[0]])

    pairs = None
    returned = []
    for chunk in range(chunks):
        while any(got is None for got in arrived[chunk]):
            queue.pop(0)()
        if chunk == 0:
            pairs = nodes(pack, pace[1])
        made = tree(pairs, dmats, arrived[chunk])
        returned.append([made[0]] + [None] * (rows - 1))
        queue += near_trades(returned[chunk], made)
        for k in far:
            if queue:
                queue.pop(0)()
            returned[chunk][k] = far_swap(made[k], k)
    while queue:
        queue.pop(0)()

    out = None
    for chunk in range(chunks):
        groups = [[0] + near, far]
        if chunk == chunks - 1:
            groups = [[0] + near, far[:cut]] + [[k] for k in far[cut:]]
        for ks in groups:
            ks = [k for k in ks if k < rows]
            if not ks:
                continue
            held = {}
            for k in ks:
                held.setdefault(id(inners[chunk, k][0]), []).append(k)
            for some in held.values():
                inner, begin = inners[chunk, some[0]]
                out = last(chunk, some, inner, begin, [returned[chunk][k] for k in some], out)
    return out


def solution(mesh):
    placed = (
        P("row", "col"),
        P(None, ("row", "col"), None),
        P(None, "row", None),
        P(None, "row", None),
        P(None, "row", None),
    )
    return jax.shard_map(
        local, mesh=mesh, in_specs=placed, out_specs=P("row", "col"), check_vma=False
    )
```

```python
import functools

import jax
import jax.numpy as jnp
from jax import lax
from jax.experimental import pallas as pl
from jax.experimental.pallas import tpu as pltpu
from jax.sharding import PartitionSpec as P

VMEM_LIMIT = 16 * 1024 * 1024
LARGE_LIMIT = 56 * 1024 * 1024
F32 = jnp.float32
BF16 = jnp.bfloat16
FLIGHT = 3
NEEDS = {3: ["leaf"], 5: [(0, 0)], 6: [(0, 1)], 7: [(0, 2), (1, 0)], 8: [(1, 1)], 9: [(1, 2)], 12: [(2, 0)], 13: [(2, 1)], 14: [(2, 2)], 15: [(3, 0), (3, 1)]}
RIDE = 0
PACE = (0, 2, 4)
CHUNKS = 2


def mm(left, right):
    return jnp.dot(left, right, precision=lax.Precision.HIGHEST, preferred_element_type=F32)


def halves(value):
    high = value.astype(BF16)
    return high, (value - high.astype(F32)).astype(BF16)


def mm3(left, right):
    high, low = halves(right)

    def dot(a, b):
        return jnp.dot(a, b, preferred_element_type=F32)

    return dot(left[0], high) + (dot(left[0], low) + dot(left[1], high))


def params(limit=VMEM_LIMIT):
    return pltpu.CompilerParams(vmem_limit_bytes=limit)


def cost(flops, nbytes):
    return pl.CostEstimate(flops=int(flops), bytes_accessed=int(nbytes), transcendentals=0)


def prep_kernel(vecs_ref, leaf_ref, after_ref, rows_ref, send_ref, rest_ref, dmat_ref):
    width = leaf_ref.shape[-1]

    def put(ref, place, value):
        high, low = halves(value)
        ref[(0, *place)] = high
        ref[(1, *place)] = low

    one, two = vecs_ref[0], vecs_ref[1]
    one_top, one_rest = one[:width], one[width:]
    two_top, two_rest = two[:width], two[width:]
    first, second = leaf_ref[0].T, leaf_ref[1].T
    two_rest_t, two_top_t = two_rest.T, two_top.T
    zero = jnp.zeros((width, width), F32)
    left, right, both = slice(0, width), slice(width, 2 * width), slice(None)
    cross = mm(two_rest_t, one_rest)
    lower = -mm(second, mm(cross, first))
    top_l, rest_l = mm(two_top, second), mm(two_rest, second)
    put(rows_ref, (left, both), one.T)
    put(rows_ref, (right, left), zero)
    put(rows_ref, (right, slice(width, None)), two_rest_t)
    put(send_ref, (left, left), -mm(one_top, first))
    put(send_ref, (left, right), zero)
    put(send_ref, (right, left), mm(two_top, lower))
    put(send_ref, (right, right), top_l)
    put(rest_ref, (both, left), mm(one_rest, first) + mm(two_rest, lower))
    put(rest_ref, (both, right), rest_l)
    put(rest_ref, (both, slice(2 * width, None)), mm(rest_l, two_top_t))
    shape = (width, width)
    eye = lax.broadcasted_iota(jnp.int32, shape, 0) == lax.broadcasted_iota(jnp.int32, shape, 1)
    dmat_ref[...] = eye.astype(F32) - mm(top_l, two_top_t)


def pack_kernel(place_ref, vecs_ref, t_ref, out_ref):
    panels = vecs_ref.shape[0]
    share = out_ref.shape[1] // (2 * panels)
    part = pl.ds(pl.multiple_of(place_ref[1] * share, share), share)
    for panel in range(panels):
        out_ref[0, pl.ds(2 * panel * share, share), :] = vecs_ref[panel, part, :]
        out_ref[0, pl.ds((2 * panel + 1) * share, share), :] = t_ref[panel, part, :]


def touch_kernel(*refs):
    refs[-1][...] = refs[0][...]


def leaf_kernel(parts, place_ref, window_ref, rows_ref, send_ref, after_ref, inner_ref, *refs):
    pieces, (buffer, sems) = refs[: len(parts)], refs[len(parts) :]
    width = send_ref.shape[1] // 2
    copies = []
    for i, part in enumerate(parts):
        copy = pltpu.make_async_copy(part(place_ref, window_ref), buffer.at[i], sems.at[i])
        copy.start()
        copies.append(copy)
    for i, piece in enumerate(pieces):
        copies[i].wait()
        inner = mm3((rows_ref[0], rows_ref[1]), buffer[i])
        inner_ref[i] = inner
        message = mm3((send_ref[0], send_ref[1]), inner)
        piece[:width, :] = message[:width] + buffer[i, :width, :]
        piece[width:, :] = message[width:]


def nodes_kernel(place_ref, after_ref, pack_ref, pair_ref):
    width = pair_ref.shape[-1] // 2

    def whole(i):
        parts = pack_ref.shape[0]
        share = width // parts
        return jnp.concatenate(
            [pack_ref[c ^ place_ref[1], 0, i * share : (i + 1) * share] for c in range(parts)], axis=0
        )

    def put(panel, rows, columns, value):
        high, low = halves(value)
        pair_ref[0, panel, 0, rows, columns] = high
        pair_ref[1, panel, 0, rows, columns] = low

    top, low = slice(0, width), slice(width, 2 * width)
    panels = pair_ref.shape[1]
    for panel in range(panels):
        vfac = whole(2 * panel)
        sfac_t = whole(2 * panel + 1).T
        right = mm(sfac_t, vfac.T)
        put(panel, top, top, sfac_t)
        put(panel, top, low, right)
        put(panel, low, top, mm(vfac, sfac_t))
        put(panel, low, low, mm(vfac, right))


def tree_kernel(rows, order, place_ref, pair_ref, dmat_ref, *refs):
    pieces, outs = [None] * rows, [None] * rows
    for i, k in enumerate(order):
        pieces[k] = refs[i]
        outs[k] = refs[rows + i]
    first, second = refs[2 * rows :]
    width = first.shape[1]
    me = place_ref[0]
    levels = rows.bit_length() - 1
    for k in range(rows):
        first[me ^ k] = pieces[k][:width, :]
        second[me ^ k] = pieces[k][width:, :]

    def each(count, body):
        if rows <= 8:
            for j in range(count):
                body(j, 0)
        else:
            lax.fori_loop(0, count, body, 0)

    def sweep(panel, tops):
        for level in range(levels):
            stride = 1 << level

            def pair(j, carry, level=level, stride=stride):
                a = (j >> level << (level + 1)) + (j & (stride - 1))
                b = a + stride
                top_a, top_b = tops[a], tops[b]
                both = jnp.concatenate([top_a, top_b], axis=0)
                change = mm3((pair_ref[0, panel, b], pair_ref[1, panel, b]), both)
                tops[a] = top_a - change[:width]
                tops[b] = top_b - change[width:]
                return carry

            each(rows // 2, pair)
        root = tops[0]
        low = slice(width, 2 * width)
        tops[0] = root - mm3((pair_ref[0, panel, 0, low, low], pair_ref[1, panel, 0, low, low]), root)

    def leaf(r, carry):
        dmat = jnp.concatenate([dmat_ref[c ^ place_ref[1], me ^ r] for c in range(dmat_ref.shape[0])], axis=0)
        second[r] = mm3(halves(dmat), first[r]) - second[r]
        return carry

    sweep(0, first)
    each(rows, leaf)
    sweep(1, second)
    for k in range(rows):
        outs[k][:width, :] = first[me ^ k]
        outs[k][width:, :] = second[me ^ k]


def last_kernel(parts, begin, place_ref, window_ref, inner_ref, rest_ref, *refs):
    count = len(parts)
    pieces, (out_ref, buffer, both, sems) = refs[:count], refs[-4:]
    width = inner_ref.shape[1] // 2
    loads, stores = [], []
    for i, part in enumerate(parts):
        source = part(place_ref, window_ref).at[pl.ds(width, window_ref.shape[-2] - width)]
        loads.append(pltpu.make_async_copy(source, buffer.at[i, pl.ds(width, source.shape[0])], sems.at[0, i]))
        stores.append(pltpu.make_async_copy(buffer.at[i], part(place_ref, out_ref), sems.at[1, i]))
    for load in loads:
        load.start()
    for i, piece in enumerate(pieces):
        both[: 2 * width, :] = inner_ref[begin + i]
        both[2 * width :, :] = piece[:width, :]
        change = mm3((rest_ref[0], rest_ref[1]), both[...])
        buffer[i, :width, :] = piece[width:, :]
        loads[i].wait()
        buffer[i, width:, :] = buffer[i, width:, :] - change
        stores[i].start()
    for store in stores:
        store.wait()


def vmem():
    return pl.BlockSpec(memory_space=pltpu.VMEM)


def anywhere():
    return pl.BlockSpec(memory_space=pl.ANY)


def smem():
    return pl.BlockSpec(memory_space=pltpu.SMEM)


def hbm():
    return pl.BlockSpec(memory_space=pltpu.HBM)


def corner(value):
    return value[(0,) * (value.ndim - 2)][:8, :128]


def swap(value, axis, k):
    return lax.ppermute(value, axis, [(i, i ^ k) for i in range(lax.axis_size(axis))])


def butterfly(window, leaf_vecs, leaf_t, node_vecs, node_t):
    width, panels = leaf_t.shape[-1], leaf_t.shape[0]
    rows = lax.axis_size("row")
    me = lax.axis_index("row")
    work = window
    all_rows = lax.all_gather(leaf_vecs, "col", axis=1, tiled=True)
    for panel in range(panels):
        vecs = all_rows[panel]
        work = work - mm(vecs, mm(leaf_t[panel].T, mm(vecs.T, work)))
        top, vfac, sfac = work[:width], node_vecs[panel], node_t[panel]
        for level in range(rows.bit_length() - 1):
            lower = me // (1 << level) % 2 == 0
            got, got_v, got_s = (swap(value, "row", 1 << level) for value in (top, vfac, sfac))
            top_a, top_b = jnp.where(lower, top, got), jnp.where(lower, got, top)
            use_v, use_s = jnp.where(lower, got_v, vfac), jnp.where(lower, got_s, sfac)
            weight = mm(use_s.T, top_a + mm(use_v.T, top_b))
            top = jnp.where(lower, top_a - weight, top_b - mm(use_v, weight))
        root = top - mm(vfac, mm(sfac.T, mm(vfac.T, top)))
        work = jnp.concatenate([jnp.where(me == 0, root, top), work[width:]], axis=0)
    return work


def local(window, leaf_vecs, leaf_t, node_vecs, node_t):
    rows, cols = lax.axis_size("row"), lax.axis_size("col")
    width = leaf_t.shape[-1]
    panels = leaf_t.shape[0]
    height, ncols = window.shape
    chunks = CHUNKS if ncols % (CHUNKS * rows * 128) == 0 else 1
    span = ncols // chunks
    n = span // rows
    if n % 128 or panels != 2 or rows < 4:
        return butterfly(window, leaf_vecs, leaf_t, node_vecs, node_t)
    me = lax.axis_index("row").astype(jnp.int32)
    col = lax.axis_index("col").astype(jnp.int32)
    parts = 2 if cols % 2 == 0 else 1
    core = col % parts
    place = jnp.stack([me, core])

    vecs = lax.all_gather(leaf_vecs, "col", axis=1, tiled=True)
    share = width // parts
    pack = pl.pallas_call(
        pack_kernel,
        out_shape=jax.ShapeDtypeStruct((1, 2 * panels * share, width), F32),
        in_specs=[smem(), vmem(), vmem()],
        out_specs=vmem(),
        compiler_params=params(),
        cost_estimate=cost(0, 2**20),
        name="pack",
    )(place, node_vecs, node_t)
    steps = []
    for k in [1 << bit for bit in reversed(range(rows.bit_length() - 1))]:
        steps.append(swap(pack, "row", k))
        pack = jnp.stack([pack, steps[-1]], axis=1).reshape(-1, *pack.shape[1:])

    rows_m, send_m, rest_m, dmat = pl.pallas_call(
        prep_kernel,
        out_shape=(
            jax.ShapeDtypeStruct((2, 2 * width, height), BF16),
            jax.ShapeDtypeStruct((2, 2 * width, 2 * width), BF16),
            jax.ShapeDtypeStruct((2, height - width, 3 * width), BF16),
            jax.ShapeDtypeStruct((width, width), F32),
        ),
        in_specs=[vmem(), vmem(), vmem()],
        out_specs=(vmem(),) * 4,
        compiler_params=params(),
        cost_estimate=cost(40 * width**3 * 6, 2**21),
        name="prep",
    )(vecs, leaf_t, steps[0])

    def part(chunk, k):
        return lambda place, ref: ref.at[:, pl.ds(pl.multiple_of((chunk * rows + (place[0] ^ k)) * n, n), n)]

    def touch(value, after):
        if not after:
            return value
        after = [corner(array) for array in after]
        return pl.pallas_call(
            touch_kernel,
            out_shape=jax.ShapeDtypeStruct(value.shape, value.dtype),
            in_specs=[vmem()] * (1 + len(after)),
            out_specs=vmem(),
            input_output_aliases={0: 0},
            compiler_params=params(),
            cost_estimate=cost(0, 0),
            name="touch",
        )(value, *after)

    def leaf(chunk, ks, after):
        count = len(ks)
        out = pl.pallas_call(
            functools.partial(leaf_kernel, [part(chunk, k) for k in ks]),
            in_specs=[smem(), hbm(), vmem(), vmem(), vmem()],
            out_specs=(vmem(),) * (1 + count),
            scratch_shapes=[pltpu.VMEM((count, height, n), F32), pltpu.SemaphoreType.DMA((count,))],
            out_shape=(jax.ShapeDtypeStruct((count, 2 * width, n), F32),)
            + (jax.ShapeDtypeStruct((2 * width, n), F32),) * count,
            compiler_params=params(LARGE_LIMIT if chunk == 0 and ks[0] == far[0] else VMEM_LIMIT),
            cost_estimate=cost(
                2 * 2 * width * (height + 2 * width) * n * count * 3, 4 * n * count * (height + 4 * width)
            ),
            name="leaf",
        )(place, window, rows_m, send_m, corner(after))
        return out[0], list(out[1:])

    def nodes(pack, after):
        return pl.pallas_call(
            nodes_kernel,
            grid_spec=pltpu.PrefetchScalarGridSpec(
                num_scalar_prefetch=1,
                grid=(rows,),
                in_specs=[
                    pl.BlockSpec(after.shape, lambda r, place: (0, 0)),
                    pl.BlockSpec((parts, 1, *pack.shape[2:]), lambda r, place: (0, r ^ place[0], 0, 0)),
                ],
                out_specs=pl.BlockSpec((2, panels, 1, 2 * width, 2 * width), lambda r, place: (0, 0, r, 0, 0)),
            ),
            out_shape=jax.ShapeDtypeStruct((2, panels, rows, 2 * width, 2 * width), BF16),
            compiler_params=params(),
            cost_estimate=cost(rows * 12 * width**3 * 6, 2**23),
            name="nodes",
        )(place, after, pack)

    def tree(pairs, dmats, pieces):
        out = pl.pallas_call(
            functools.partial(tree_kernel, rows, order),
            out_shape=(jax.ShapeDtypeStruct((2 * width, n), F32),) * rows,
            in_specs=[smem()] + [vmem()] * (2 + rows),
            out_specs=(vmem(),) * rows,
            scratch_shapes=[pltpu.VMEM((rows, width, n), F32)] * 2,
            compiler_params=params(),
            cost_estimate=cost(rows * 8 * 4 * width * width * n * 3, 2**23),
            name="tree",
        )(place, pairs, dmats, *[pieces[k] for k in order])
        return [out[order.index(k)] for k in range(rows)]

    def last(chunk, ks, inner, begin, pieces, out):
        count = len(ks)
        operands = [place, window, inner, rest_m, *pieces]
        in_specs = [smem(), hbm()] + [vmem()] * (2 + count)
        aliases = {}
        if out is not None:
            in_specs.append(hbm())
            aliases = {len(operands): 0}
            operands.append(out)
        return pl.pallas_call(
            functools.partial(last_kernel, [part(chunk, k) for k in ks], begin),
            in_specs=in_specs,
            out_specs=hbm(),
            scratch_shapes=[
                pltpu.VMEM((count, height, n), F32),
                pltpu.VMEM((3 * width, n), F32),
                pltpu.SemaphoreType.DMA((2, count)),
            ],
            out_shape=jax.ShapeDtypeStruct(window.shape, F32),
            input_output_aliases=aliases,
            compiler_params=params(),
            cost_estimate=cost(
                2 * 3 * width * (height - width) * n * count * 3, 4 * n * count * (2 * height + 4 * width)
            ),
            name="last",
        )(*operands)

    half = rows // 2
    far, near = list(range(half, rows)), list(range(1, half))
    order = far + near + [0]
    cut = max(1, half // 2)

    inners, sent = {}, [[None] * rows for _ in range(chunks)]

    def leaves(chunk, ks, after):
        inner, made = leaf(chunk, ks, after)
        for i, k in enumerate(ks):
            inners[chunk, k] = inner, i
            sent[chunk][k] = made[i]
        return inner

    ride = far[RIDE]
    flat = share
    groups = max(1, n // width)
    extra = flat * width // n

    def fold(pack):
        return jnp.concatenate([pack[g * extra : (g + 1) * extra] for g in range(groups)], axis=1)

    def unfold(rider):
        return jnp.concatenate([rider[:, g * width : (g + 1) * width] for g in range(groups)], axis=0)

    fars, nears = [], {}

    def far_swap(value, k):
        after = fars[len(fars) - FLIGHT :][:1] if len(fars) >= FLIGHT else []
        after += [nears[key] for key in NEEDS.get(len(fars), ()) if key in nears]
        fars.append(swap(touch(value, after), "row", k))
        return fars[-1]

    def near_trades(stage, got, pieces):
        for i, k in enumerate(near):
            got[k] = nears[stage, i] = swap(pieces[k], "row", k)

    arrived = [[None] * rows for _ in range(chunks)]
    own = other = None
    for chunk in range(chunks):
        if chunk == 0:
            after = leaves(0, far[:1], send_m)
            leaves(0, far[1:], steps[min(1, len(steps) - 1)])
        else:
            leaves(chunk, far, fars[1])
            leaves(chunk, [0] + near, nears[0, len(near) - 1])
            arrived[chunk][0] = sent[chunk][0]
            near_trades(chunk, arrived[chunk], sent[chunk])
        for k in far:
            if (chunk, k) == (0, ride):
                own = fold(lax.dynamic_slice_in_dim(dmat, core * share, share, axis=0))
                got = far_swap(jnp.concatenate([sent[0][k], own]), k)
                arrived[0][k], other = got[: 2 * width], got[2 * width :]
                nears["leaf"] = leaves(0, [0] + near, steps[-1])
                arrived[0][0] = sent[0][0]
                for j in near:
                    sent[0][j] = jnp.concatenate([sent[0][j], own, other])
                near_trades(0, arrived[0], sent[0])
            else:
                arrived[chunk][k] = far_swap(sent[chunk][k], k)

    shares = {0: own, ride: other}
    for k in near:
        got = arrived[0][k]
        arrived[0][k] = got[: 2 * width]
        shares[k], shares[k ^ ride] = got[2 * width : 2 * width + extra], got[2 * width + extra :]
    shares = jnp.stack([unfold(shares[k]) for k in range(rows)])
    def join(value, after):
        if parts == 1:
            return value[None]
        return jnp.stack([value, swap(touch(value, after), "col", 1)])

    pace = [fars[min(i, len(fars) - 1)] for i in PACE]
    dmats = join(shares, [pace[2]])
    pack = join(pack, [pace[0]])

    pairs = None
    returned = []
    for chunk in range(chunks):
        if chunk == 0:
            pairs = nodes(pack, corner(pace[1]))
        made = tree(pairs, dmats, arrived[chunk])
        returned.append([made[0]] + [None] * (rows - 1))
        near_trades(chunks + chunk, returned[chunk], made)
        for k in far:
            returned[chunk][k] = far_swap(made[k], k)

    out = None
    for chunk in range(chunks):
        groups = [[0] + near, far]
        if chunk == chunks - 1:
            groups = [[0] + near, far[:cut]] + [[k] for k in far[cut:]]
        for ks in groups:
            ks = [k for k in ks if k < rows]
            if not ks:
                continue
            held = {}
            for k in ks:
                held.setdefault(id(inners[chunk, k][0]), []).append(k)
            for some in held.values():
                inner, begin = inners[chunk, some[0]]
                out = last(chunk, some, inner, begin, [returned[chunk][k] for k in some], out)
    return out


def solution(mesh):
    placed = (
        P("row", "col"),
        P(None, ("row", "col"), None),
        P(None, "row", None),
        P(None, "row", None),
        P(None, "row", None),
    )
    return jax.shard_map(
        local, mesh=mesh, in_specs=placed, out_specs=P("row", "col"), check_vma=False
    )
```

```python
import functools

import jax
import jax.numpy as jnp
from jax import lax
from jax.experimental import pallas as pl
from jax.experimental.pallas import tpu as pltpu
from jax.sharding import PartitionSpec as P

VMEM_LIMIT = 16 * 1024 * 1024
LARGE_LIMIT = 56 * 1024 * 1024
F32 = jnp.float32
BF16 = jnp.bfloat16
FLIGHT = 3
NEEDS = {3: ["leaf"], 5: [(0, 0)], 6: [(0, 1)], 7: [(0, 2), (1, 0)], 8: [(1, 1)], 9: [(1, 2)], 12: [(2, 0)], 13: [(2, 1)], 14: [(2, 2)], 15: [(3, 0), (3, 1)]}
RIDE = 0
PACE = (0, 2, 4)
CHUNKS = 2


def mm(left, right):
    return jnp.dot(left, right, precision=lax.Precision.HIGHEST, preferred_element_type=F32)


def halves(value):
    high = value.astype(BF16)
    return high, (value - high.astype(F32)).astype(BF16)


def mm3(left, right):
    high, low = halves(right)

    def dot(a, b):
        return jnp.dot(a, b, preferred_element_type=F32)

    return dot(left[0], high) + (dot(left[0], low) + dot(left[1], high))


def params(limit=VMEM_LIMIT):
    return pltpu.CompilerParams(vmem_limit_bytes=limit)


def cost(flops, nbytes):
    return pl.CostEstimate(flops=int(flops), bytes_accessed=int(nbytes), transcendentals=0)


def prep_kernel(vecs_ref, leaf_ref, after_ref, rows_ref, send_ref, rest_ref, dmat_ref):
    width = leaf_ref.shape[-1]

    def put(ref, place, value):
        high, low = halves(value)
        ref[(0, *place)] = high
        ref[(1, *place)] = low

    one, two = vecs_ref[0], vecs_ref[1]
    one_top, one_rest = one[:width], one[width:]
    two_top, two_rest = two[:width], two[width:]
    first, second = leaf_ref[0].T, leaf_ref[1].T
    two_rest_t, two_top_t = two_rest.T, two_top.T
    zero = jnp.zeros((width, width), F32)
    left, right, both = slice(0, width), slice(width, 2 * width), slice(None)
    cross = mm(two_rest_t, one_rest)
    lower = -mm(second, mm(cross, first))
    top_l, rest_l = mm(two_top, second), mm(two_rest, second)
    put(rows_ref, (left, both), one.T)
    put(rows_ref, (right, left), zero)
    put(rows_ref, (right, slice(width, None)), two_rest_t)
    put(send_ref, (left, left), -mm(one_top, first))
    put(send_ref, (left, right), zero)
    put(send_ref, (right, left), mm(two_top, lower))
    put(send_ref, (right, right), top_l)
    put(rest_ref, (both, left), mm(one_rest, first) + mm(two_rest, lower))
    put(rest_ref, (both, right), rest_l)
    put(rest_ref, (both, slice(2 * width, None)), mm(rest_l, two_top_t))
    shape = (width, width)
    eye = lax.broadcasted_iota(jnp.int32, shape, 0) == lax.broadcasted_iota(jnp.int32, shape, 1)
    dmat_ref[...] = eye.astype(F32) - mm(top_l, two_top_t)


def pack_kernel(place_ref, vecs_ref, t_ref, out_ref):
    panels = vecs_ref.shape[0]
    share = out_ref.shape[1] // (2 * panels)
    part = pl.ds(pl.multiple_of(place_ref[1] * share, share), share)
    for panel in range(panels):
        out_ref[0, pl.ds(2 * panel * share, share), :] = vecs_ref[panel, part, :]
        out_ref[0, pl.ds((2 * panel + 1) * share, share), :] = t_ref[panel, part, :]


def touch_kernel(*refs):
    refs[-1][...] = refs[0][...]


def leaf_kernel(parts, place_ref, window_ref, rows_ref, send_ref, after_ref, inner_ref, *refs):
    pieces, (buffer, sems) = refs[: len(parts)], refs[len(parts) :]
    width = send_ref.shape[1] // 2
    copies = []
    for i, part in enumerate(parts):
        copy = pltpu.make_async_copy(part(place_ref, window_ref), buffer.at[i], sems.at[i])
        copy.start()
        copies.append(copy)
    for i, piece in enumerate(pieces):
        copies[i].wait()
        inner = mm3((rows_ref[0], rows_ref[1]), buffer[i])
        inner_ref[i] = inner
        message = mm3((send_ref[0], send_ref[1]), inner)
        piece[:width, :] = message[:width] + buffer[i, :width, :]
        piece[width : 2 * width, :] = message[width:]
        extra = piece.shape[0] - 2 * width
        for g in range(piece.shape[1] // width if extra else 0):
            begin = place_ref[1] * (extra * piece.shape[1] // width) + g * extra
            part = after_ref[pl.ds(pl.multiple_of(begin, 8), extra), :]
            piece[2 * width :, g * width : (g + 1) * width] = part


def nodes_kernel(place_ref, after_ref, pack_ref, pair_ref):
    width = pair_ref.shape[-1] // 2

    def whole(i):
        parts = pack_ref.shape[0]
        share = width // parts
        return jnp.concatenate(
            [pack_ref[c ^ place_ref[1], 0, i * share : (i + 1) * share] for c in range(parts)], axis=0
        )

    def put(panel, rows, columns, value):
        high, low = halves(value)
        pair_ref[0, panel, 0, rows, columns] = high
        pair_ref[1, panel, 0, rows, columns] = low

    top, low = slice(0, width), slice(width, 2 * width)
    panels = pair_ref.shape[1]
    for panel in range(panels):
        vfac = whole(2 * panel)
        sfac_t = whole(2 * panel + 1).T
        right = mm(sfac_t, vfac.T)
        put(panel, top, top, sfac_t)
        put(panel, top, low, right)
        put(panel, low, top, mm(vfac, sfac_t))
        put(panel, low, low, mm(vfac, right))


def tree_kernel(rows, order, place_ref, pair_ref, dmat_ref, *refs):
    pieces, outs = [None] * rows, [None] * rows
    for i, k in enumerate(order):
        pieces[k] = refs[i]
        outs[k] = refs[rows + i]
    first, second = refs[2 * rows :]
    width = first.shape[1]
    me = place_ref[0]
    levels = rows.bit_length() - 1
    for k in range(rows):
        first[me ^ k] = pieces[k][:width, :]
        second[me ^ k] = pieces[k][width:, :]

    def each(count, body):
        if rows <= 8:
            for j in range(count):
                body(j, 0)
        else:
            lax.fori_loop(0, count, body, 0)

    def sweep(panel, tops):
        for level in range(levels):
            stride = 1 << level

            def pair(j, carry, level=level, stride=stride):
                a = (j >> level << (level + 1)) + (j & (stride - 1))
                b = a + stride
                top_a, top_b = tops[a], tops[b]
                both = jnp.concatenate([top_a, top_b], axis=0)
                change = mm3((pair_ref[0, panel, b], pair_ref[1, panel, b]), both)
                tops[a] = top_a - change[:width]
                tops[b] = top_b - change[width:]
                return carry

            each(rows // 2, pair)
        root = tops[0]
        low = slice(width, 2 * width)
        tops[0] = root - mm3((pair_ref[0, panel, 0, low, low], pair_ref[1, panel, 0, low, low]), root)

    def leaf(r, carry):
        dmat = jnp.concatenate([dmat_ref[c ^ place_ref[1], me ^ r] for c in range(dmat_ref.shape[0])], axis=0)
        second[r] = mm3(halves(dmat), first[r]) - second[r]
        return carry

    sweep(0, first)
    each(rows, leaf)
    sweep(1, second)
    for k in range(rows):
        outs[k][:width, :] = first[me ^ k]
        outs[k][width:, :] = second[me ^ k]


def last_kernel(parts, begin, place_ref, window_ref, inner_ref, rest_ref, *refs):
    count = len(parts)
    pieces, (out_ref, buffer, both, sems) = refs[:count], refs[-4:]
    width = inner_ref.shape[1] // 2
    loads, stores = [], []
    for i, part in enumerate(parts):
        source = part(place_ref, window_ref).at[pl.ds(width, window_ref.shape[-2] - width)]
        loads.append(pltpu.make_async_copy(source, buffer.at[i, pl.ds(width, source.shape[0])], sems.at[0, i]))
        stores.append(pltpu.make_async_copy(buffer.at[i], part(place_ref, out_ref), sems.at[1, i]))
    for load in loads:
        load.start()
    for i, piece in enumerate(pieces):
        both[: 2 * width, :] = inner_ref[begin + i]
        both[2 * width :, :] = piece[:width, :]
        change = mm3((rest_ref[0], rest_ref[1]), both[...])
        buffer[i, :width, :] = piece[width:, :]
        loads[i].wait()
        buffer[i, width:, :] = buffer[i, width:, :] - change
        stores[i].start()
    for store in stores:
        store.wait()


def vmem():
    return pl.BlockSpec(memory_space=pltpu.VMEM)


def anywhere():
    return pl.BlockSpec(memory_space=pl.ANY)


def smem():
    return pl.BlockSpec(memory_space=pltpu.SMEM)


def hbm():
    return pl.BlockSpec(memory_space=pltpu.HBM)


def corner(value):
    return value[(0,) * (value.ndim - 2)][:8, :128]


def swap(value, axis, k):
    return lax.ppermute(value, axis, [(i, i ^ k) for i in range(lax.axis_size(axis))])


def butterfly(window, leaf_vecs, leaf_t, node_vecs, node_t):
    width, panels = leaf_t.shape[-1], leaf_t.shape[0]
    rows = lax.axis_size("row")
    me = lax.axis_index("row")
    work = window
    all_rows = lax.all_gather(leaf_vecs, "col", axis=1, tiled=True)
    for panel in range(panels):
        vecs = all_rows[panel]
        work = work - mm(vecs, mm(leaf_t[panel].T, mm(vecs.T, work)))
        top, vfac, sfac = work[:width], node_vecs[panel], node_t[panel]
        for level in range(rows.bit_length() - 1):
            lower = me // (1 << level) % 2 == 0
            got, got_v, got_s = (swap(value, "row", 1 << level) for value in (top, vfac, sfac))
            top_a, top_b = jnp.where(lower, top, got), jnp.where(lower, got, top)
            use_v, use_s = jnp.where(lower, got_v, vfac), jnp.where(lower, got_s, sfac)
            weight = mm(use_s.T, top_a + mm(use_v.T, top_b))
            top = jnp.where(lower, top_a - weight, top_b - mm(use_v, weight))
        root = top - mm(vfac, mm(sfac.T, mm(vfac.T, top)))
        work = jnp.concatenate([jnp.where(me == 0, root, top), work[width:]], axis=0)
    return work


def local(window, leaf_vecs, leaf_t, node_vecs, node_t):
    rows, cols = lax.axis_size("row"), lax.axis_size("col")
    width = leaf_t.shape[-1]
    panels = leaf_t.shape[0]
    height, ncols = window.shape
    chunks = CHUNKS if ncols % (CHUNKS * rows * 128) == 0 else 1
    span = ncols // chunks
    n = span // rows
    if n % 128 or panels != 2 or rows < 4:
        return butterfly(window, leaf_vecs, leaf_t, node_vecs, node_t)
    me = lax.axis_index("row").astype(jnp.int32)
    col = lax.axis_index("col").astype(jnp.int32)
    parts = 2 if cols % 2 == 0 else 1
    core = col % parts
    place = jnp.stack([me, core])

    vecs = lax.all_gather(leaf_vecs, "col", axis=1, tiled=True)
    share = width // parts
    pack = pl.pallas_call(
        pack_kernel,
        out_shape=jax.ShapeDtypeStruct((1, 2 * panels * share, width), F32),
        in_specs=[smem(), vmem(), vmem()],
        out_specs=vmem(),
        compiler_params=params(),
        cost_estimate=cost(0, 2**20),
        name="pack",
    )(place, node_vecs, node_t)
    steps = []
    for k in [1 << bit for bit in reversed(range(rows.bit_length() - 1))]:
        steps.append(swap(pack, "row", k))
        pack = jnp.stack([pack, steps[-1]], axis=1).reshape(-1, *pack.shape[1:])

    rows_m, send_m, rest_m, dmat = pl.pallas_call(
        prep_kernel,
        out_shape=(
            jax.ShapeDtypeStruct((2, 2 * width, height), BF16),
            jax.ShapeDtypeStruct((2, 2 * width, 2 * width), BF16),
            jax.ShapeDtypeStruct((2, height - width, 3 * width), BF16),
            jax.ShapeDtypeStruct((width, width), F32),
        ),
        in_specs=[vmem(), vmem(), vmem()],
        out_specs=(vmem(),) * 4,
        compiler_params=params(),
        cost_estimate=cost(40 * width**3 * 6, 2**21),
        name="prep",
    )(vecs, leaf_t, steps[0])

    def part(chunk, k):
        return lambda place, ref: ref.at[:, pl.ds(pl.multiple_of((chunk * rows + (place[0] ^ k)) * n, n), n)]

    def touch(value, after):
        if not after:
            return value
        after = [corner(array) for array in after]
        return pl.pallas_call(
            touch_kernel,
            out_shape=jax.ShapeDtypeStruct(value.shape, value.dtype),
            in_specs=[vmem()] * (1 + len(after)),
            out_specs=vmem(),
            input_output_aliases={0: 0},
            compiler_params=params(),
            cost_estimate=cost(0, 0),
            name="touch",
        )(value, *after)

    def leaf(chunk, ks, after, rider):
        count = len(ks)
        out = pl.pallas_call(
            functools.partial(leaf_kernel, [part(chunk, k) for k in ks]),
            in_specs=[smem(), hbm(), vmem(), vmem(), vmem()],
            out_specs=(vmem(),) * (1 + count),
            scratch_shapes=[pltpu.VMEM((count, height, n), F32), pltpu.SemaphoreType.DMA((count,))],
            out_shape=(jax.ShapeDtypeStruct((count, 2 * width, n), F32),)
            + (jax.ShapeDtypeStruct((2 * width + rider, n), F32),) * count,
            compiler_params=params(LARGE_LIMIT if chunk == 0 and ks[0] == far[0] else VMEM_LIMIT),
            cost_estimate=cost(
                2 * 2 * width * (height + 2 * width) * n * count * 3, 4 * n * count * (height + 4 * width)
            ),
            name="leaf",
        )(place, window, rows_m, send_m, after if rider else corner(after))
        return out[0], list(out[1:])

    def nodes(pack, after):
        return pl.pallas_call(
            nodes_kernel,
            grid_spec=pltpu.PrefetchScalarGridSpec(
                num_scalar_prefetch=1,
                grid=(rows,),
                in_specs=[
                    pl.BlockSpec(after.shape, lambda r, place: (0, 0)),
                    pl.BlockSpec((parts, 1, *pack.shape[2:]), lambda r, place: (0, r ^ place[0], 0, 0)),
                ],
                out_specs=pl.BlockSpec((2, panels, 1, 2 * width, 2 * width), lambda r, place: (0, 0, r, 0, 0)),
            ),
            out_shape=jax.ShapeDtypeStruct((2, panels, rows, 2 * width, 2 * width), BF16),
            compiler_params=params(),
            cost_estimate=cost(rows * 12 * width**3 * 6, 2**23),
            name="nodes",
        )(place, after, pack)

    def tree(pairs, dmats, pieces):
        out = pl.pallas_call(
            functools.partial(tree_kernel, rows, order),
            out_shape=(jax.ShapeDtypeStruct((2 * width, n), F32),) * rows,
            in_specs=[smem()] + [vmem()] * (2 + rows),
            out_specs=(vmem(),) * rows,
            scratch_shapes=[pltpu.VMEM((rows, width, n), F32)] * 2,
            compiler_params=params(),
            cost_estimate=cost(rows * 8 * 4 * width * width * n * 3, 2**23),
            name="tree",
        )(place, pairs, dmats, *[pieces[k] for k in order])
        return [out[order.index(k)] for k in range(rows)]

    def last(chunk, ks, inner, begin, pieces, out):
        count = len(ks)
        operands = [place, window, inner, rest_m, *pieces]
        in_specs = [smem(), hbm()] + [vmem()] * (2 + count)
        aliases = {}
        if out is not None:
            in_specs.append(hbm())
            aliases = {len(operands): 0}
            operands.append(out)
        return pl.pallas_call(
            functools.partial(last_kernel, [part(chunk, k) for k in ks], begin),
            in_specs=in_specs,
            out_specs=hbm(),
            scratch_shapes=[
                pltpu.VMEM((count, height, n), F32),
                pltpu.VMEM((3 * width, n), F32),
                pltpu.SemaphoreType.DMA((2, count)),
            ],
            out_shape=jax.ShapeDtypeStruct(window.shape, F32),
            input_output_aliases=aliases,
            compiler_params=params(),
            cost_estimate=cost(
                2 * 3 * width * (height - width) * n * count * 3, 4 * n * count * (2 * height + 4 * width)
            ),
            name="last",
        )(*operands)

    half = rows // 2
    far, near = list(range(half, rows)), list(range(1, half))
    order = far + near + [0]
    cut = max(1, half // 2)

    inners, sent = {}, [[None] * rows for _ in range(chunks)]

    def leaves(chunk, ks, after, rider=0):
        inner, made = leaf(chunk, ks, after, rider)
        for i, k in enumerate(ks):
            inners[chunk, k] = inner, i
            sent[chunk][k] = made[i]
        return inner

    ride = far[RIDE]
    flat = share
    groups = max(1, n // width)
    extra = flat * width // n

    def unfold(rider):
        return jnp.concatenate([rider[:, g * width : (g + 1) * width] for g in range(groups)], axis=0)

    fars, nears = [], {}

    def far_swap(value, k):
        after = fars[len(fars) - FLIGHT :][:1] if len(fars) >= FLIGHT else []
        after += [nears[key] for key in NEEDS.get(len(fars), ()) if key in nears]
        fars.append(swap(touch(value, after), "row", k))
        return fars[-1]

    def near_trades(stage, got, pieces):
        for i, k in enumerate(near):
            got[k] = nears[stage, i] = swap(pieces[k], "row", k)

    arrived = [[None] * rows for _ in range(chunks)]
    own = other = None
    for chunk in range(chunks):
        if chunk == 0:
            after = leaves(0, far[:1], dmat, extra)
            leaves(0, far[1:], steps[min(1, len(steps) - 1)])
        else:
            leaves(chunk, far, fars[1])
            leaves(chunk, [0] + near, nears[0, len(near) - 1])
            arrived[chunk][0] = sent[chunk][0]
            near_trades(chunk, arrived[chunk], sent[chunk])
        for k in far:
            if (chunk, k) == (0, ride):
                own = sent[0][k][2 * width :]
                got = far_swap(sent[0][k], k)
                arrived[0][k], other = got[: 2 * width], got[2 * width :]
                nears["leaf"] = leaves(0, [0] + near, steps[-1])
                arrived[0][0] = sent[0][0]
                for j in near:
                    sent[0][j] = jnp.concatenate([sent[0][j], own, other])
                near_trades(0, arrived[0], sent[0])
            else:
                arrived[chunk][k] = far_swap(sent[chunk][k], k)

    shares = {0: own, ride: other}
    for k in near:
        got = arrived[0][k]
        arrived[0][k] = got[: 2 * width]
        shares[k], shares[k ^ ride] = got[2 * width : 2 * width + extra], got[2 * width + extra :]
    shares = jnp.stack([unfold(shares[k]) for k in range(rows)])
    def join(value, after):
        if parts == 1:
            return value[None]
        return jnp.stack([value, swap(touch(value, after), "col", 1)])

    pace = [fars[min(i, len(fars) - 1)] for i in PACE]
    dmats = join(shares, [pace[2]])
    pack = join(pack, [pace[0]])

    pairs = None
    returned = []
    for chunk in range(chunks):
        if chunk == 0:
            pairs = nodes(pack, corner(pace[1]))
        made = tree(pairs, dmats, arrived[chunk])
        returned.append([made[0]] + [None] * (rows - 1))
        near_trades(chunks + chunk, returned[chunk], made)
        for k in far:
            returned[chunk][k] = far_swap(made[k], k)

    out = None
    for chunk in range(chunks):
        groups = [[0] + near, far]
        if chunk == chunks - 1:
            groups = [[0] + near, far[:cut]] + [[k] for k in far[cut:]]
        for ks in groups:
            ks = [k for k in ks if k < rows]
            if not ks:
                continue
            held = {}
            for k in ks:
                held.setdefault(id(inners[chunk, k][0]), []).append(k)
            for some in held.values():
                inner, begin = inners[chunk, some[0]]
                out = last(chunk, some, inner, begin, [returned[chunk][k] for k in some], out)
    return out


def solution(mesh):
    placed = (
        P("row", "col"),
        P(None, ("row", "col"), None),
        P(None, "row", None),
        P(None, "row", None),
        P(None, "row", None),
    )
    return jax.shard_map(
        local, mesh=mesh, in_specs=placed, out_specs=P("row", "col"), check_vma=False
    )
```

```python
import functools

import jax
import jax.numpy as jnp
from jax import lax
from jax.experimental import pallas as pl
from jax.experimental.pallas import tpu as pltpu
from jax.sharding import PartitionSpec as P

VMEM_LIMIT = 16 * 1024 * 1024
LARGE_LIMIT = 56 * 1024 * 1024
F32 = jnp.float32
BF16 = jnp.bfloat16
FLIGHT = 3
NEEDS = {3: ["leaf"], 5: [(0, 0)], 6: [(0, 1)], 7: [(0, 2), (1, 0)], 8: [(1, 1)], 9: [(1, 2)], 12: [(2, 0)], 13: [(2, 1)], 14: [(2, 2)], 15: [(3, 0), (3, 1), "last"]}
RIDE = 0
PACE = (0, 2, 4)
CHUNKS = 2


def mm(left, right):
    return jnp.dot(left, right, precision=lax.Precision.HIGHEST, preferred_element_type=F32)


def halves(value):
    high = value.astype(BF16)
    return high, (value - high.astype(F32)).astype(BF16)


def mm3(left, right):
    high, low = halves(right)

    def dot(a, b):
        return jnp.dot(a, b, preferred_element_type=F32)

    return dot(left[0], high) + (dot(left[0], low) + dot(left[1], high))


def params(limit=VMEM_LIMIT):
    return pltpu.CompilerParams(vmem_limit_bytes=limit)


def cost(flops, nbytes):
    return pl.CostEstimate(flops=int(flops), bytes_accessed=int(nbytes), transcendentals=0)


def prep_kernel(vecs_ref, leaf_ref, after_ref, rows_ref, send_ref, rest_ref, dmat_ref):
    width = leaf_ref.shape[-1]

    def put(ref, place, value):
        high, low = halves(value)
        ref[(0, *place)] = high
        ref[(1, *place)] = low

    one, two = vecs_ref[0], vecs_ref[1]
    one_top, one_rest = one[:width], one[width:]
    two_top, two_rest = two[:width], two[width:]
    first, second = leaf_ref[0].T, leaf_ref[1].T
    two_rest_t, two_top_t = two_rest.T, two_top.T
    zero = jnp.zeros((width, width), F32)
    left, right, both = slice(0, width), slice(width, 2 * width), slice(None)
    cross = mm(two_rest_t, one_rest)
    lower = -mm(second, mm(cross, first))
    top_l, rest_l = mm(two_top, second), mm(two_rest, second)
    put(rows_ref, (left, both), one.T)
    put(rows_ref, (right, left), zero)
    put(rows_ref, (right, slice(width, None)), two_rest_t)
    put(send_ref, (left, left), -mm(one_top, first))
    put(send_ref, (left, right), zero)
    put(send_ref, (right, left), mm(two_top, lower))
    put(send_ref, (right, right), top_l)
    put(rest_ref, (both, left), mm(one_rest, first) + mm(two_rest, lower))
    put(rest_ref, (both, right), rest_l)
    put(rest_ref, (both, slice(2 * width, None)), mm(rest_l, two_top_t))
    shape = (width, width)
    eye = lax.broadcasted_iota(jnp.int32, shape, 0) == lax.broadcasted_iota(jnp.int32, shape, 1)
    dmat_ref[...] = eye.astype(F32) - mm(top_l, two_top_t)


def pack_kernel(place_ref, vecs_ref, t_ref, out_ref):
    panels = vecs_ref.shape[0]
    share = out_ref.shape[1] // (2 * panels)
    part = pl.ds(pl.multiple_of(place_ref[1] * share, share), share)
    for panel in range(panels):
        out_ref[0, pl.ds(2 * panel * share, share), :] = vecs_ref[panel, part, :]
        out_ref[0, pl.ds((2 * panel + 1) * share, share), :] = t_ref[panel, part, :]


def touch_kernel(*refs):
    refs[-1][...] = refs[0][...]


def leaf_kernel(parts, place_ref, window_ref, rows_ref, send_ref, after_ref, inner_ref, *refs):
    pieces, (buffer, sems) = refs[: len(parts)], refs[len(parts) :]
    width = send_ref.shape[1] // 2
    copies = []
    for i, part in enumerate(parts):
        copy = pltpu.make_async_copy(part(place_ref, window_ref), buffer.at[i], sems.at[i])
        copy.start()
        copies.append(copy)
    for i, piece in enumerate(pieces):
        copies[i].wait()
        inner = mm3((rows_ref[0], rows_ref[1]), buffer[i])
        inner_ref[i] = inner
        message = mm3((send_ref[0], send_ref[1]), inner)
        piece[:width, :] = message[:width] + buffer[i, :width, :]
        piece[width : 2 * width, :] = message[width:]
        extra = piece.shape[0] - 2 * width
        for g in range(piece.shape[1] // width if extra else 0):
            begin = place_ref[1] * (extra * piece.shape[1] // width) + g * extra
            part = after_ref[pl.ds(pl.multiple_of(begin, 8), extra), :]
            piece[2 * width :, g * width : (g + 1) * width] = part


def nodes_kernel(place_ref, after_ref, pack_ref, pair_ref):
    width = pair_ref.shape[-1] // 2

    def whole(i):
        parts = pack_ref.shape[0]
        share = width // parts
        return jnp.concatenate(
            [pack_ref[c ^ place_ref[1], 0, i * share : (i + 1) * share] for c in range(parts)], axis=0
        )

    def put(panel, rows, columns, value):
        high, low = halves(value)
        pair_ref[0, panel, 0, rows, columns] = high
        pair_ref[1, panel, 0, rows, columns] = low

    top, low = slice(0, width), slice(width, 2 * width)
    panels = pair_ref.shape[1]
    for panel in range(panels):
        vfac = whole(2 * panel)
        sfac_t = whole(2 * panel + 1).T
        right = mm(sfac_t, vfac.T)
        put(panel, top, top, sfac_t)
        put(panel, top, low, right)
        put(panel, low, top, mm(vfac, sfac_t))
        put(panel, low, low, mm(vfac, right))


def tree_kernel(rows, order, place_ref, pair_ref, dmat_ref, *refs):
    pieces, outs = [None] * rows, [None] * rows
    for i, k in enumerate(order):
        pieces[k] = refs[i]
        outs[k] = refs[rows + i]
    first, second = refs[2 * rows :]
    width = first.shape[1]
    me = place_ref[0]
    levels = rows.bit_length() - 1
    for k in range(rows):
        first[me ^ k] = pieces[k][:width, :]
        second[me ^ k] = pieces[k][width:, :]

    def each(count, body):
        if rows <= 8:
            for j in range(count):
                body(j, 0)
        else:
            lax.fori_loop(0, count, body, 0)

    def sweep(panel, tops):
        for level in range(levels):
            stride = 1 << level

            def pair(j, carry, level=level, stride=stride):
                a = (j >> level << (level + 1)) + (j & (stride - 1))
                b = a + stride
                top_a, top_b = tops[a], tops[b]
                both = jnp.concatenate([top_a, top_b], axis=0)
                change = mm3((pair_ref[0, panel, b], pair_ref[1, panel, b]), both)
                tops[a] = top_a - change[:width]
                tops[b] = top_b - change[width:]
                return carry

            each(rows // 2, pair)
        root = tops[0]
        low = slice(width, 2 * width)
        tops[0] = root - mm3((pair_ref[0, panel, 0, low, low], pair_ref[1, panel, 0, low, low]), root)

    def leaf(r, carry):
        dmat = jnp.concatenate([dmat_ref[c ^ place_ref[1], me ^ r] for c in range(dmat_ref.shape[0])], axis=0)
        second[r] = mm3(halves(dmat), first[r]) - second[r]
        return carry

    sweep(0, first)
    each(rows, leaf)
    sweep(1, second)
    for k in range(rows):
        outs[k][:width, :] = first[me ^ k]
        outs[k][width:, :] = second[me ^ k]


def last_kernel(parts, begin, place_ref, window_ref, inner_ref, rest_ref, *refs):
    count = len(parts)
    pieces, (out_ref, token_ref, buffer, both, sems) = refs[:count], refs[-5:]
    token_ref[...] = jnp.zeros(token_ref.shape, F32)
    width = inner_ref.shape[1] // 2
    loads, stores = [], []
    for i, part in enumerate(parts):
        source = part(place_ref, window_ref).at[pl.ds(width, window_ref.shape[-2] - width)]
        loads.append(pltpu.make_async_copy(source, buffer.at[i, pl.ds(width, source.shape[0])], sems.at[0, i]))
        stores.append(pltpu.make_async_copy(buffer.at[i], part(place_ref, out_ref), sems.at[1, i]))
    for load in loads:
        load.start()
    for i, piece in enumerate(pieces):
        both[: 2 * width, :] = inner_ref[begin + i]
        both[2 * width :, :] = piece[:width, :]
        change = mm3((rest_ref[0], rest_ref[1]), both[...])
        buffer[i, :width, :] = piece[width:, :]
        loads[i].wait()
        buffer[i, width:, :] = buffer[i, width:, :] - change
        stores[i].start()
    for store in stores:
        store.wait()


def vmem():
    return pl.BlockSpec(memory_space=pltpu.VMEM)


def anywhere():
    return pl.BlockSpec(memory_space=pl.ANY)


def smem():
    return pl.BlockSpec(memory_space=pltpu.SMEM)


def hbm():
    return pl.BlockSpec(memory_space=pltpu.HBM)


def corner(value):
    return value[(0,) * (value.ndim - 2)][:8, :128]


def swap(value, axis, k):
    return lax.ppermute(value, axis, [(i, i ^ k) for i in range(lax.axis_size(axis))])


def butterfly(window, leaf_vecs, leaf_t, node_vecs, node_t):
    width, panels = leaf_t.shape[-1], leaf_t.shape[0]
    rows = lax.axis_size("row")
    me = lax.axis_index("row")
    work = window
    all_rows = lax.all_gather(leaf_vecs, "col", axis=1, tiled=True)
    for panel in range(panels):
        vecs = all_rows[panel]
        work = work - mm(vecs, mm(leaf_t[panel].T, mm(vecs.T, work)))
        top, vfac, sfac = work[:width], node_vecs[panel], node_t[panel]
        for level in range(rows.bit_length() - 1):
            lower = me // (1 << level) % 2 == 0
            got, got_v, got_s = (swap(value, "row", 1 << level) for value in (top, vfac, sfac))
            top_a, top_b = jnp.where(lower, top, got), jnp.where(lower, got, top)
            use_v, use_s = jnp.where(lower, got_v, vfac), jnp.where(lower, got_s, sfac)
            weight = mm(use_s.T, top_a + mm(use_v.T, top_b))
            top = jnp.where(lower, top_a - weight, top_b - mm(use_v, weight))
        root = top - mm(vfac, mm(sfac.T, mm(vfac.T, top)))
        work = jnp.concatenate([jnp.where(me == 0, root, top), work[width:]], axis=0)
    return work


def local(window, leaf_vecs, leaf_t, node_vecs, node_t):
    rows, cols = lax.axis_size("row"), lax.axis_size("col")
    width = leaf_t.shape[-1]
    panels = leaf_t.shape[0]
    height, ncols = window.shape
    chunks = CHUNKS if ncols % (CHUNKS * rows * 128) == 0 else 1
    span = ncols // chunks
    n = span // rows
    if n % 128 or panels != 2 or rows < 4:
        return butterfly(window, leaf_vecs, leaf_t, node_vecs, node_t)
    me = lax.axis_index("row").astype(jnp.int32)
    col = lax.axis_index("col").astype(jnp.int32)
    parts = 2 if cols % 2 == 0 else 1
    core = col % parts
    place = jnp.stack([me, core])

    vecs = lax.all_gather(leaf_vecs, "col", axis=1, tiled=True)
    share = width // parts
    pack = pl.pallas_call(
        pack_kernel,
        out_shape=jax.ShapeDtypeStruct((1, 2 * panels * share, width), F32),
        in_specs=[smem(), vmem(), vmem()],
        out_specs=vmem(),
        compiler_params=params(),
        cost_estimate=cost(0, 2**20),
        name="pack",
    )(place, node_vecs, node_t)
    steps = []
    for k in [1 << bit for bit in reversed(range(rows.bit_length() - 1))]:
        steps.append(swap(pack, "row", k))
        pack = jnp.stack([pack, steps[-1]], axis=1).reshape(-1, *pack.shape[1:])

    rows_m, send_m, rest_m, dmat = pl.pallas_call(
        prep_kernel,
        out_shape=(
            jax.ShapeDtypeStruct((2, 2 * width, height), BF16),
            jax.ShapeDtypeStruct((2, 2 * width, 2 * width), BF16),
            jax.ShapeDtypeStruct((2, height - width, 3 * width), BF16),
            jax.ShapeDtypeStruct((width, width), F32),
        ),
        in_specs=[vmem(), vmem(), vmem()],
        out_specs=(vmem(),) * 4,
        compiler_params=params(),
        cost_estimate=cost(40 * width**3 * 6, 2**21),
        name="prep",
    )(vecs, leaf_t, steps[0])

    def part(chunk, k):
        return lambda place, ref: ref.at[:, pl.ds(pl.multiple_of((chunk * rows + (place[0] ^ k)) * n, n), n)]

    def touch(value, after):
        if not after:
            return value
        after = [corner(array) for array in after]
        return pl.pallas_call(
            touch_kernel,
            out_shape=jax.ShapeDtypeStruct(value.shape, value.dtype),
            in_specs=[vmem()] * (1 + len(after)),
            out_specs=vmem(),
            input_output_aliases={0: 0},
            compiler_params=params(),
            cost_estimate=cost(0, 0),
            name="touch",
        )(value, *after)

    def leaf(chunk, ks, after, rider):
        count = len(ks)
        out = pl.pallas_call(
            functools.partial(leaf_kernel, [part(chunk, k) for k in ks]),
            in_specs=[smem(), hbm(), vmem(), vmem(), vmem()],
            out_specs=(vmem(),) * (1 + count),
            scratch_shapes=[pltpu.VMEM((count, height, n), F32), pltpu.SemaphoreType.DMA((count,))],
            out_shape=(jax.ShapeDtypeStruct((count, 2 * width, n), F32),)
            + (jax.ShapeDtypeStruct((2 * width + rider, n), F32),) * count,
            compiler_params=params(LARGE_LIMIT if chunk == 0 and ks[0] == far[0] else VMEM_LIMIT),
            cost_estimate=cost(
                2 * 2 * width * (height + 2 * width) * n * count * 3, 4 * n * count * (height + 4 * width)
            ),
            name="leaf",
        )(place, window, rows_m, send_m, after if rider else corner(after))
        return out[0], list(out[1:])

    def nodes(pack, after):
        return pl.pallas_call(
            nodes_kernel,
            grid_spec=pltpu.PrefetchScalarGridSpec(
                num_scalar_prefetch=1,
                grid=(rows,),
                in_specs=[
                    pl.BlockSpec(after.shape, lambda r, place: (0, 0)),
                    pl.BlockSpec((parts, 1, *pack.shape[2:]), lambda r, place: (0, r ^ place[0], 0, 0)),
                ],
                out_specs=pl.BlockSpec((2, panels, 1, 2 * width, 2 * width), lambda r, place: (0, 0, r, 0, 0)),
            ),
            out_shape=jax.ShapeDtypeStruct((2, panels, rows, 2 * width, 2 * width), BF16),
            compiler_params=params(),
            cost_estimate=cost(rows * 12 * width**3 * 6, 2**23),
            name="nodes",
        )(place, after, pack)

    def tree(pairs, dmats, pieces):
        out = pl.pallas_call(
            functools.partial(tree_kernel, rows, order),
            out_shape=(jax.ShapeDtypeStruct((2 * width, n), F32),) * rows,
            in_specs=[smem()] + [vmem()] * (2 + rows),
            out_specs=(vmem(),) * rows,
            scratch_shapes=[pltpu.VMEM((rows, width, n), F32)] * 2,
            compiler_params=params(),
            cost_estimate=cost(rows * 8 * 4 * width * width * n * 3, 2**23),
            name="tree",
        )(place, pairs, dmats, *[pieces[k] for k in order])
        return [out[order.index(k)] for k in range(rows)]

    def last(chunk, ks, inner, begin, pieces, out):
        count = len(ks)
        operands = [place, window, inner, rest_m, *pieces]
        in_specs = [smem(), hbm()] + [vmem()] * (2 + count)
        aliases = {}
        if out is not None:
            in_specs.append(hbm())
            aliases = {len(operands): 0}
            operands.append(out)
        return pl.pallas_call(
            functools.partial(last_kernel, [part(chunk, k) for k in ks], begin),
            in_specs=in_specs,
            out_specs=(hbm(), vmem()),
            scratch_shapes=[
                pltpu.VMEM((count, height, n), F32),
                pltpu.VMEM((3 * width, n), F32),
                pltpu.SemaphoreType.DMA((2, count)),
            ],
            out_shape=(jax.ShapeDtypeStruct(window.shape, F32), jax.ShapeDtypeStruct((8, 128), F32)),
            input_output_aliases=aliases,
            compiler_params=params(),
            cost_estimate=cost(
                2 * 3 * width * (height - width) * n * count * 3, 4 * n * count * (2 * height + 4 * width)
            ),
            name="last",
        )(*operands)

    half = rows // 2
    far, near = list(range(half, rows)), list(range(1, half))
    order = far + near + [0]
    cut = max(1, half // 2)

    inners, sent = {}, [[None] * rows for _ in range(chunks)]

    def leaves(chunk, ks, after, rider=0):
        inner, made = leaf(chunk, ks, after, rider)
        for i, k in enumerate(ks):
            inners[chunk, k] = inner, i
            sent[chunk][k] = made[i]
        return inner

    ride = far[RIDE]
    flat = share
    groups = max(1, n // width)
    extra = flat * width // n

    def unfold(rider):
        return jnp.concatenate([rider[:, g * width : (g + 1) * width] for g in range(groups)], axis=0)

    fars, nears = [], {}

    def far_swap(value, k):
        after = fars[len(fars) - FLIGHT :][:1] if len(fars) >= FLIGHT else []
        after += [nears[key] for key in NEEDS.get(len(fars), ()) if key in nears]
        fars.append(swap(touch(value, after), "row", k))
        return fars[-1]

    def near_trades(stage, got, pieces):
        for i, k in enumerate(near):
            got[k] = nears[stage, i] = swap(pieces[k], "row", k)

    arrived = [[None] * rows for _ in range(chunks)]
    own = other = None
    for chunk in range(chunks):
        if chunk == 0:
            after = leaves(0, far[:1], dmat, extra)
            leaves(0, far[1:], steps[min(1, len(steps) - 1)])
        else:
            leaves(chunk, far, fars[1])
            leaves(chunk, [0] + near, nears[0, len(near) - 1])
            arrived[chunk][0] = sent[chunk][0]
            near_trades(chunk, arrived[chunk], sent[chunk])
        for k in far:
            if (chunk, k) == (0, ride):
                own = sent[0][k][2 * width :]
                got = far_swap(sent[0][k], k)
                arrived[0][k], other = got[: 2 * width], got[2 * width :]
                nears["leaf"] = leaves(0, [0] + near, steps[-1])
                arrived[0][0] = sent[0][0]
                for j in near:
                    sent[0][j] = jnp.concatenate([sent[0][j], own, other])
                near_trades(0, arrived[0], sent[0])
            else:
                arrived[chunk][k] = far_swap(sent[chunk][k], k)

    shares = {0: own, ride: other}
    for k in near:
        got = arrived[0][k]
        arrived[0][k] = got[: 2 * width]
        shares[k], shares[k ^ ride] = got[2 * width : 2 * width + extra], got[2 * width + extra :]
    shares = jnp.stack([unfold(shares[k]) for k in range(rows)])
    def join(value, after):
        if parts == 1:
            return value[None]
        return jnp.stack([value, swap(touch(value, after), "col", 1)])

    pace = [fars[min(i, len(fars) - 1)] for i in PACE]
    dmats = join(shares, [pace[2]])
    pack = join(pack, [pace[0]])

    def finish(chunk, ks, out):
        made = {}
        for k in ks:
            made.setdefault(id(inners[chunk, k][0]), []).append(k)
        for some in made.values():
            inner, begin = inners[chunk, some[0]]
            out, nears["last"] = last(chunk, some, inner, begin, [returned[chunk][k] for k in some], out)
        return out

    pairs = out = None
    returned = []
    for chunk in range(chunks):
        if chunk == 0:
            pairs = nodes(pack, corner(pace[1]))
        made = tree(pairs, dmats, arrived[chunk])
        returned.append([made[0]] + [None] * (rows - 1))
        near_trades(chunks + chunk, returned[chunk], made)
        for k in far:
            if chunk and k == far[-1]:
                out = finish(chunk - 1, [0] + near, out)
                out = finish(chunk - 1, far, out)
            returned[chunk][k] = far_swap(made[k], k)
    out = finish(chunks - 1, [0] + near, out)
    out = finish(chunks - 1, far[:cut], out)
    for k in far[cut:]:
        out = finish(chunks - 1, [k], out)
    return out


def solution(mesh):
    placed = (
        P("row", "col"),
        P(None, ("row", "col"), None),
        P(None, "row", None),
        P(None, "row", None),
        P(None, "row", None),
    )
    return jax.shard_map(
        local, mesh=mesh, in_specs=placed, out_specs=P("row", "col"), check_vma=False
    )
```
